32 devices in a mesh: row: 4 (over x, core), col: 8 (over z, y).
Axes of the slice: x: 2, y: 2, z: 4, core: 2. Of those that a mesh axis runs over, the one named last changes fastest.
Arguments:
- tiles: float32 [4, 8, 128, 128, 128], P('row', 'col'), may hold values from -0.125 to 0.125
- tile_rows: int32 [4, 8, 128], P('row', 'col'), may hold values from 0 to 31, as said below
- tile_cols: int32 [4, 8, 128], P('row', 'col'), may hold values from 0 to 15, as said below
- tile_counts: int32 [4, 8], P('row', 'col'), may hold values from 1 to 128, as said below
- vectors: float32 [8, 16384], P(None, ('row', 'col')), may hold values from -6 to 6
Outputs:
- product: float32 [8, 16384], P(None, ('row', 'col'))
The draws below stay inside these ranges and needn't reach their ends.
Inputs may be any that keep to these rules, and one draw needn't show every extreme that they name: `tile_counts`: each device has 1 to 128 live slots; the target count of grid row r is the ceiling of 128 * (r + 1) / 4 less a jitter of 0 to 32, at least 1; one device of the last grid row has exactly 128. `tile_rows`: live slots of a device name distinct tiles on or below the block diagonal (global block row at least global block column); slots past the count hold 0. `tile_cols`: drawn together with tile_rows; slots past the count hold 0.
All inputs are finite; a program needn't handle non-finite values.
Results may differ from the reference program's by a relative error of at most 0.0003.
Values sent between devices are 32-bit elements; how exact they have to be, the bound alone decides.
A program may use at most 64 MiB of HBM per device.

```python
import jax
import jax.numpy as jnp
from jax import lax

TILE = 128
VECS = 8
TILES_DEV = 128
BLOCKS_DEV = 4
ROW_BLOCKS = 32
COL_BLOCKS = 16
DIM = 16384
N_ROW = 4
N_COL = 8


def pattern(key):
    row_blocks = N_COL * BLOCKS_DEV
    col_blocks = N_ROW * BLOCKS_DEV
    cells = row_blocks * col_blocks
    cell = jnp.arange(cells, dtype=jnp.int32)
    local_row = cell // col_blocks
    local_col = cell % col_blocks
    devices = N_ROW * N_COL
    spread = max(2 ** 30 // cells, 2)

    def one(device, sub):
        grid_row = device // N_COL
        grid_col = device % N_COL
        big_row = grid_row * row_blocks + local_row
        big_col = (local_col // BLOCKS_DEV * N_COL + grid_col) * BLOCKS_DEV + local_col % BLOCKS_DEV
        lower = big_row >= big_col
        scores = jax.random.randint(sub, (cells,), 0, spread, dtype=jnp.int32) * cells + cell
        scores = jnp.where(lower, scores, -1 - cell)
        unused, picked = lax.top_k(scores, TILES_DEV)
        return (picked.astype(jnp.int32), jnp.sum(lower.astype(jnp.int32)))
    base_key = jax.random.fold_in(key, 11)
    keys = jax.random.split(base_key, devices)
    index = jnp.arange(devices, dtype=jnp.int32)
    picked, avail = jax.vmap(one)(index, keys)
    grid_row = index // N_COL
    grid_col = index % N_COL
    base = (TILES_DEV * (grid_row + 1) + N_ROW - 1) // N_ROW
    jitter = jax.random.randint(jax.random.fold_in(key, 12), (devices,), 0, TILES_DEV // 4 + 1, dtype=jnp.int32)
    target = jnp.maximum(base - jitter, 1)
    chosen = jax.random.randint(jax.random.fold_in(key, 13), (), 0, N_COL, dtype=jnp.int32)
    target = jnp.where((grid_row == N_ROW - 1) & (grid_col == chosen), TILES_DEV, target)
    count = jnp.minimum(target, avail).astype(jnp.int32)
    valid = jnp.arange(TILES_DEV, dtype=jnp.int32)[None, :] < count[:, None]
    rows = jnp.where(valid, picked // col_blocks, 0).astype(jnp.int32)
    cols = jnp.where(valid, picked % col_blocks, 0).astype(jnp.int32)
    return (rows.reshape(N_ROW, N_COL, TILES_DEV), cols.reshape(N_ROW, N_COL, TILES_DEV), count.reshape(N_ROW, N_COL))


def draw_tile_rows(key, part):
    return pattern(key)[0]


def draw_tile_cols(key, part):
    return pattern(key)[1]


def draw_tile_counts(key, part):
    return pattern(key)[2]


def block_levels(own_key, dims, cuts, least, largest):
    level, own = 1.0, jax.random.fold_in(own_key, 6)
    for position, parts in cuts:
        steps = jnp.exp(jax.random.uniform(jax.random.fold_in(own, position), (parts,), jnp.float32, least / len(cuts), largest / len(cuts)))
        level = level * jnp.repeat(steps, dims[position] // parts).reshape([-1 if axis == position else 1 for axis in range(len(dims))])
    return level


def noise(rng, extent, scale, reach, cuts=(), kind=jnp.bfloat16):
    result = scale * jax.random.normal(rng, extent, jnp.float32)
    if cuts:
        result = result * block_levels(rng, extent, cuts, -0.22, 0.18)
    return jnp.clip(result, -reach, reach).astype(kind)


def setup_inputs(seed: int = 0) -> dict:
    seeds = jax.random.split(jax.random.key(seed), 6)
    tiles = noise(seeds[0], (N_ROW, N_COL, TILES_DEV, TILE, TILE), (TILE * 16) ** -0.5, 0.125, ((0, 4), (1, 8)), jnp.float32)
    tile_rows = draw_tile_rows(jax.random.fold_in(seeds[5], 71), 0)
    tile_cols = draw_tile_cols(jax.random.fold_in(seeds[5], 71), 0)
    tile_counts = draw_tile_counts(jax.random.fold_in(seeds[5], 71), 0)
    vectors = noise(seeds[4], (VECS, DIM), 1.0, 6.0, ((1, 32),), jnp.float32)
    return {"tiles": tiles, "tile_rows": tile_rows, "tile_cols": tile_cols, "tile_counts": tile_counts, "vectors": vectors}


def device_terms(blocks, rows, cols, count, row_inputs, col_inputs):
    valid = jnp.arange(TILES_DEV, dtype=jnp.int32) < count
    from_cols = jnp.take(col_inputs, cols, axis=1)
    from_rows = jnp.take(row_inputs, rows, axis=1)
    first = jnp.einsum('tab,ktb->kta', blocks, from_cols, precision=lax.Precision.HIGHEST)
    second = jnp.einsum('tab,kta->ktb', blocks, from_rows, precision=lax.Precision.HIGHEST)
    row_hits = ((rows[:, None] == jnp.arange(ROW_BLOCKS, dtype=jnp.int32)[None, :]) & valid[:, None]).astype(blocks.dtype)
    col_hits = ((cols[:, None] == jnp.arange(COL_BLOCKS, dtype=jnp.int32)[None, :]) & valid[:, None]).astype(blocks.dtype)
    row_part = jnp.einsum('kta,ti->kia', first, row_hits, precision=lax.Precision.HIGHEST)
    col_part = jnp.einsum('ktb,tj->kjb', second, col_hits, precision=lax.Precision.HIGHEST)
    return row_part, col_part


def reference(tiles, tile_rows, tile_cols, tile_counts, vectors):
    grid = vectors.reshape(VECS, N_ROW, N_COL, BLOCKS_DEV, TILE)
    flat_tiles = tiles.reshape(N_ROW * N_COL, TILES_DEV, TILE, TILE)
    flat_rows = tile_rows.reshape(N_ROW * N_COL, TILES_DEV)
    flat_cols = tile_cols.reshape(N_ROW * N_COL, TILES_DEV)
    flat_counts = tile_counts.reshape(N_ROW * N_COL)

    def step(total, device):
        grid_row = device // N_COL
        grid_col = device % N_COL
        row_inputs = lax.dynamic_index_in_dim(grid, grid_row, 1, keepdims=False).reshape(VECS, ROW_BLOCKS, TILE)
        col_inputs = lax.dynamic_index_in_dim(grid, grid_col, 2, keepdims=False).reshape(VECS, COL_BLOCKS, TILE)
        blocks = lax.dynamic_index_in_dim(flat_tiles, device, 0, keepdims=False)
        rows = lax.dynamic_index_in_dim(flat_rows, device, 0, keepdims=False)
        cols = lax.dynamic_index_in_dim(flat_cols, device, 0, keepdims=False)
        count = lax.dynamic_index_in_dim(flat_counts, device, 0, keepdims=False)
        row_part, col_part = device_terms(blocks, rows, cols, count, row_inputs, col_inputs)
        total = total.at[:, grid_row].add(row_part.reshape(VECS, N_COL, BLOCKS_DEV, TILE))
        total = total.at[:, :, grid_col].add(col_part.reshape(VECS, N_ROW, BLOCKS_DEV, TILE))
        return total, None

    start = jnp.zeros((VECS, N_ROW, N_COL, BLOCKS_DEV, TILE), vectors.dtype)
    total, unused = lax.scan(step, start, jnp.arange(N_ROW * N_COL, dtype=jnp.int32))
    return total.reshape(VECS, DIM)
```

```python
import functools

import jax
import jax.numpy as jnp
from jax import lax
from jax.experimental import pallas as pl
from jax.experimental.pallas import tpu as pltpu
from jax.sharding import PartitionSpec as P

MESH = pl.DeviceIdType.MESH
F32 = jnp.float32
BF16 = jnp.bfloat16
CHUNKS = 8
UNROLL = 4


def split(value):
    high = value.astype(BF16)
    low = (value - high.astype(F32)).astype(BF16)
    return high, low


def hit_matrix(labels, count, blocks, vecs):
    slots = labels.shape[1]
    slot = lax.broadcasted_iota(jnp.int32, (vecs, slots), 1)
    names = jnp.where(slot < count, jnp.broadcast_to(labels, (vecs, slots)), -1)
    source = lax.broadcasted_iota(jnp.int32, (slots, slots * vecs), 0)
    target = lax.broadcasted_iota(jnp.int32, (slots, slots * vecs), 1)
    spread = jnp.where((target >= source * vecs) & (target < source * vecs + vecs), 1.0, 0.0).astype(BF16)
    wide = jnp.dot(names.astype(F32).astype(BF16), spread, preferred_element_type=F32)[0:1]
    lane = lax.rem(lax.broadcasted_iota(jnp.int32, (1, slots * vecs), 1), vecs)
    code = wide.astype(jnp.int32) * vecs + lane
    place = lax.broadcasted_iota(jnp.int32, (blocks * vecs, slots * vecs), 0)
    return jnp.where(place == code, 1.0, 0.0).astype(BF16)


def kernel(
    rows_s, cols_s, count_s, rows_v, cols_v, x_ref, tiles_ref, out_ref,
    raw, both, col_x, row_x, col_lhs, row_lhs, row_hits, col_hits, terms, row_part, col_part, row_in, col_in,
    tile_sem, colx_send, colx_recv, rowx_send, rowx_recv, rowp_send, rowp_recv, colp_send, colp_recv,
):
    row_devices = lax.axis_size("row")
    column_devices = lax.axis_size("col")
    r = lax.axis_index("row")
    c = lax.axis_index("col")
    vecs, width = x_ref.shape
    slots, side, _ = tiles_ref.shape
    local = width // side
    row_blocks = column_devices * local
    col_blocks = row_devices * local
    chunk = slots // CHUNKS

    fetches = []
    for n in range(CHUNKS):
        piece = pl.ds(n * chunk, chunk)
        fetch = pltpu.make_async_copy(tiles_ref.at[piece], raw.at[piece], tile_sem.at[n])
        fetch.start()
        fetches.append(fetch)

    row_peers = [(lax.rem(r + d, row_devices), c) for d in range(1, row_devices)]
    col_peers = [(r, lax.rem(c + d, column_devices)) for d in range(1, column_devices)]

    barrier = pltpu.get_barrier_semaphore()
    for peer in row_peers + col_peers:
        pl.semaphore_signal(barrier, inc=1, device_id=peer, device_id_type=MESH)
    pl.semaphore_wait(barrier, len(row_peers) + len(col_peers))

    colx, rowx = [], []
    for n, peer in enumerate(row_peers):
        colx.append(pltpu.make_async_remote_copy(
            src_ref=x_ref, dst_ref=col_x.at[r], send_sem=colx_send.at[n], recv_sem=colx_recv.at[n],
            device_id=peer, device_id_type=MESH))
        colx[-1].start()
    for n, peer in enumerate(col_peers):
        rowx.append(pltpu.make_async_remote_copy(
            src_ref=x_ref, dst_ref=row_x.at[c], send_sem=rowx_send.at[n], recv_sem=rowx_recv.at[n],
            device_id=peer, device_id_type=MESH))
        rowx[-1].start()
    col_x[r] = x_ref[...]
    row_x[c] = x_ref[...]

    count = count_s[0, 0]
    row_hits[...] = hit_matrix(rows_v[...], count, row_blocks, vecs)
    col_hits[...] = hit_matrix(cols_v[...], count, col_blocks, vecs)

    for n in range(CHUNKS):
        fetches[n].wait()

        def halve(t, carry):
            high, low = split(raw[t])
            place = pl.ds(pl.multiple_of(t * side, side), side)
            both[place, 0:side] = high
            both[place, side:] = low
            return carry

        lax.fori_loop(n * chunk, (n + 1) * chunk, halve, 0, unroll=2)

    for copy in colx:
        copy.wait()
    for i in range(row_devices):
        for j in range(local):
            high, low = split(col_x[i, :, j * side:(j + 1) * side])
            n = i * local + j
            upper = jnp.concatenate([high, low], axis=0)
            under = jnp.concatenate([high, jnp.zeros_like(low)], axis=0)
            col_lhs[n, :, 0:side] = upper
            col_lhs[n, :, side:] = under

    def add_up(hits):
        high, low = split(terms[...])
        total = jnp.dot(hits[...], jnp.concatenate([high, low], axis=1), preferred_element_type=F32)
        return total[:, 0:side] + total[:, side:]

    def first(step, carry):
        for u in range(UNROLL):
            pair = step * UNROLL + u
            lhs = jnp.concatenate([col_lhs[cols_s[0, 2 * pair]], col_lhs[cols_s[0, 2 * pair + 1]]], axis=0)
            rhs = both[pl.ds(pl.multiple_of(pair * 2 * side, 2 * side), 2 * side), :]
            got = lax.dot_general(lhs, rhs, (((1,), (1,)), ((), ())), preferred_element_type=F32)
            left = got[0:2 * vecs, 0:side]
            right = got[2 * vecs:, side:]
            place = pl.multiple_of(pair * 2 * vecs, 2 * vecs)
            terms[pl.ds(place, vecs), :] = left[0:vecs] + left[vecs:]
            terms[pl.ds(place + vecs, vecs), :] = right[0:vecs] + right[vecs:]
        return carry

    lax.fori_loop(0, slots // (2 * UNROLL), first, 0)
    row_part[...] = add_up(row_hits).reshape(row_blocks, vecs, side)
    rowp = []
    for n, peer in enumerate(col_peers):
        rowp.append(pltpu.make_async_remote_copy(
            src_ref=row_part.at[pl.ds(peer[1] * local, local)], dst_ref=row_in.at[n],
            send_sem=rowp_send.at[n], recv_sem=rowp_recv.at[n], device_id=peer, device_id_type=MESH))
        rowp[-1].start()

    for copy in rowx:
        copy.wait()
    for i in range(column_devices):
        for j in range(local):
            high, low = split(row_x[i, :, j * side:(j + 1) * side])
            row_lhs[i * local + j] = jnp.concatenate([high, low], axis=0)

    def second(step, carry):
        blank = jnp.zeros((2 * vecs, side), BF16)
        for u in range(UNROLL):
            pair = step * UNROLL + u
            one = row_lhs[rows_s[0, 2 * pair]]
            two = row_lhs[rows_s[0, 2 * pair + 1]]
            lhs = jnp.concatenate([
                jnp.concatenate([one, blank], axis=1),
                jnp.concatenate([blank, two], axis=1),
            ], axis=0)
            rhs = both[pl.ds(pl.multiple_of(pair * 2 * side, 2 * side), 2 * side), :]
            got = jnp.dot(lhs, rhs, preferred_element_type=F32)
            got = got[:, 0:side] + got[:, side:]
            place = pl.multiple_of(pair * 2 * vecs, 2 * vecs)
            terms[pl.ds(place, vecs), :] = got[0:vecs] + got[vecs:2 * vecs]
            terms[pl.ds(place + vecs, vecs), :] = got[2 * vecs:3 * vecs] + got[3 * vecs:]
        return carry

    lax.fori_loop(0, slots // (2 * UNROLL), second, 0)
    col_part[...] = add_up(col_hits).reshape(col_blocks, vecs, side)
    colp = []
    for n, peer in enumerate(row_peers):
        colp.append(pltpu.make_async_remote_copy(
            src_ref=col_part.at[pl.ds(peer[0] * local, local)], dst_ref=col_in.at[n],
            send_sem=colp_send.at[n], recv_sem=colp_recv.at[n], device_id=peer, device_id_type=MESH))
        colp[-1].start()

    total = row_part[pl.ds(c * local, local)] + col_part[pl.ds(r * local, local)]
    for n, copy in enumerate(rowp):
        copy.wait()
        total += row_in[n]
    for n, copy in enumerate(colp):
        copy.wait()
        total += col_in[n]
    for j in range(local):
        out_ref[:, j * side:(j + 1) * side] = total[j]


def body(tiles, tile_rows, tile_cols, tile_counts, vectors):
    vecs, width = vectors.shape
    slots, side = tiles.shape[2:4]
    row_devices = lax.axis_size("row")
    column_devices = lax.axis_size("col")
    local = width // side
    row_blocks = column_devices * local
    col_blocks = row_devices * local
    rows = tile_rows.reshape(1, slots)
    cols = tile_cols.reshape(1, slots)
    vmem = pl.BlockSpec(memory_space=pltpu.VMEM)
    smem = pl.BlockSpec(memory_space=pltpu.SMEM)
    dma = pltpu.SemaphoreType.DMA
    return pl.pallas_call(
        kernel,
        out_shape=jax.ShapeDtypeStruct((vecs, width), F32),
        in_specs=[smem, smem, smem, vmem, vmem, vmem, pl.BlockSpec(memory_space=pl.ANY)],
        out_specs=vmem,
        scratch_shapes=[
            pltpu.VMEM((slots, side, side), F32),
            pltpu.VMEM((slots * side, 2 * side), BF16),
            pltpu.VMEM((row_devices, vecs, width), F32),
            pltpu.VMEM((column_devices, vecs, width), F32),
            pltpu.VMEM((col_blocks, 2 * vecs, 2 * side), BF16),
            pltpu.VMEM((row_blocks, 2 * vecs, side), BF16),
            pltpu.VMEM((row_blocks * vecs, slots * vecs), BF16),
            pltpu.VMEM((col_blocks * vecs, slots * vecs), BF16),
            pltpu.VMEM((slots * vecs, side), F32),
            pltpu.VMEM((row_blocks, vecs, side), F32),
            pltpu.VMEM((col_blocks, vecs, side), F32),
            pltpu.VMEM((column_devices - 1, local, vecs, side), F32),
            pltpu.VMEM((row_devices - 1, local, vecs, side), F32),
            dma((CHUNKS,)),
            dma((row_devices - 1,)),
            dma((row_devices - 1,)),
            dma((column_devices - 1,)),
            dma((column_devices - 1,)),
            dma((column_devices - 1,)),
            dma((column_devices - 1,)),
            dma((row_devices - 1,)),
            dma((row_devices - 1,)),
        ],
        compiler_params=pltpu.CompilerParams(
            collective_id=0, has_side_effects=True, vmem_limit_bytes=56 * 2**20
        ),
        cost_estimate=pl.CostEstimate(
            flops=12 * slots * side * side * vecs, bytes_accessed=4 * slots * side * side, transcendentals=0
        ),
        name="symmetric_product",
    )(rows, cols, tile_counts, rows, cols, vectors, tiles.reshape(slots, side, side))


def solution(mesh):
    in_specs = (
        P("row", "col", None, None, None),
        P("row", "col", None),
        P("row", "col", None),
        P("row", "col"),
        P(None, ("row", "col")),
    )
    out_specs = P(None, ("row", "col"))
    return jax.shard_map(body, mesh=mesh, in_specs=in_specs, out_specs=out_specs, check_vma=False)
```

```python
import functools

import jax
import jax.numpy as jnp
from jax import lax
from jax.experimental import pallas as pl
from jax.experimental.pallas import tpu as pltpu
from jax.sharding import PartitionSpec as P

MESH = pl.DeviceIdType.MESH
F32 = jnp.float32
BF16 = jnp.bfloat16
CHUNKS = 8
UNROLL = 16


def split(value):
    high = value.astype(BF16)
    low = (value - high.astype(F32)).astype(BF16)
    return high, low


def hit_matrix(labels, count, blocks, vecs):
    slots = labels.shape[1]
    slot = lax.broadcasted_iota(jnp.int32, (vecs, slots), 1)
    names = jnp.where(slot < count, jnp.broadcast_to(labels, (vecs, slots)), -1)
    source = lax.broadcasted_iota(jnp.int32, (slots, slots * vecs), 0)
    target = lax.broadcasted_iota(jnp.int32, (slots, slots * vecs), 1)
    spread = jnp.where((target >= source * vecs) & (target < source * vecs + vecs), 1.0, 0.0).astype(BF16)
    wide = jnp.dot(names.astype(F32).astype(BF16), spread, preferred_element_type=F32)[0:1]
    lane = lax.rem(lax.broadcasted_iota(jnp.int32, (1, slots * vecs), 1), vecs)
    code = wide.astype(jnp.int32) * vecs + lane
    place = lax.broadcasted_iota(jnp.int32, (blocks * vecs, slots * vecs), 0)
    return jnp.where(place == code, 1.0, 0.0).astype(BF16)


def kernel(
    rows_ref, cols_ref, count_ref, x_ref, tiles_ref, out_ref,
    rows_s, cols_s, count_s, rows_v, cols_v, raw, both, col_x, row_x, col_lhs, row_lhs, row_hits, col_hits, terms, row_part, col_part, row_in, col_in,
    small_sem, tile_sem, colx_send, colx_recv, rowx_send, rowx_recv, rowp_send, rowp_recv, colp_send, colp_recv,
):
    row_devices = lax.axis_size("row")
    column_devices = lax.axis_size("col")
    r = lax.axis_index("row")
    c = lax.axis_index("col")
    vecs, width = x_ref.shape
    slots, side, _ = tiles_ref.shape
    local = width // side
    row_blocks = column_devices * local
    col_blocks = row_devices * local
    chunk = slots // CHUNKS

    row_peers = [(lax.rem(r + d, row_devices), c) for d in range(1, row_devices)]
    col_peers = [(r, lax.rem(c + d, column_devices)) for d in range(1, column_devices)]

    barrier = pltpu.get_barrier_semaphore()
    for peer in row_peers + col_peers:
        pl.semaphore_signal(barrier, inc=1, device_id=peer, device_id_type=MESH)

    smalls = [
        pltpu.make_async_copy(source, target, small_sem.at[n])
        for n, (source, target) in enumerate([
            (rows_ref, rows_v), (cols_ref, cols_v), (count_ref, count_s), (rows_ref, rows_s), (cols_ref, cols_s),
            (x_ref, col_x.at[r]), (x_ref, row_x.at[c]),
        ])
    ]
    for copy in smalls:
        copy.start()
    fetches = []
    for n in range(CHUNKS):
        piece = pl.ds(n * chunk, chunk)
        fetch = pltpu.make_async_copy(tiles_ref.at[piece], raw.at[piece], tile_sem.at[n])
        fetch.start()
        fetches.append(fetch)
    pl.semaphore_wait(barrier, len(row_peers) + len(col_peers))

    colx, rowx = [], []
    for n, peer in enumerate(row_peers):
        colx.append(pltpu.make_async_remote_copy(
            src_ref=x_ref, dst_ref=col_x.at[r], send_sem=colx_send.at[n], recv_sem=colx_recv.at[n],
            device_id=peer, device_id_type=MESH))
        colx[-1].start()
    for n, peer in enumerate(col_peers):
        rowx.append(pltpu.make_async_remote_copy(
            src_ref=x_ref, dst_ref=row_x.at[c], send_sem=rowx_send.at[n], recv_sem=rowx_recv.at[n],
            device_id=peer, device_id_type=MESH))
        rowx[-1].start()
    for copy in smalls:
        copy.wait()
    count = count_s[0, 0]
    row_hits[...] = hit_matrix(rows_v[...], count, row_blocks, vecs)
    col_hits[...] = hit_matrix(cols_v[...], count, col_blocks, vecs)

    for n in range(CHUNKS):
        fetches[n].wait()

        def halve(t, carry):
            high, low = split(raw[t])
            place = pl.ds(pl.multiple_of(t * side, side), side)
            both[place, 0:side] = high
            both[place, side:] = low
            return carry

        lax.fori_loop(n * chunk, (n + 1) * chunk, halve, 0, unroll=8)

    for copy in colx:
        copy.wait()
    for i in range(row_devices):
        for j in range(local):
            high, low = split(col_x[i, :, j * side:(j + 1) * side])
            n = i * local + j
            upper = jnp.concatenate([high, low], axis=0)
            under = jnp.concatenate([high, jnp.zeros_like(low)], axis=0)
            col_lhs[n, :, 0:side] = upper
            col_lhs[n, :, side:] = under

    def add_up(hits):
        high, low = split(terms[...])
        total = jnp.dot(hits[...], jnp.concatenate([high, low], axis=1), preferred_element_type=F32)
        return total[:, 0:side] + total[:, side:]

    def first(step, carry):
        for u in range(UNROLL):
            pair = step * UNROLL + u
            lhs = jnp.concatenate([col_lhs[cols_s[0, 2 * pair]], col_lhs[cols_s[0, 2 * pair + 1]]], axis=0)
            rhs = both[pl.ds(pl.multiple_of(pair * 2 * side, 2 * side), 2 * side), :]
            got = lax.dot_general(lhs, rhs, (((1,), (1,)), ((), ())), preferred_element_type=F32)
            left = got[0:2 * vecs, 0:side]
            right = got[2 * vecs:, side:]
            place = pl.multiple_of(pair * 2 * vecs, 2 * vecs)
            terms[pl.ds(place, vecs), :] = left[0:vecs] + left[vecs:]
            terms[pl.ds(place + vecs, vecs), :] = right[0:vecs] + right[vecs:]
        return carry

    lax.fori_loop(0, slots // (2 * UNROLL), first, 0)
    row_part[...] = add_up(row_hits).reshape(row_blocks, vecs, side)
    rowp = []
    for n, peer in enumerate(col_peers):
        rowp.append(pltpu.make_async_remote_copy(
            src_ref=row_part.at[pl.ds(peer[1] * local, local)], dst_ref=row_in.at[n],
            send_sem=rowp_send.at[n], recv_sem=rowp_recv.at[n], device_id=peer, device_id_type=MESH))
        rowp[-1].start()

    for copy in rowx:
        copy.wait()
    for i in range(column_devices):
        for j in range(local):
            high, low = split(row_x[i, :, j * side:(j + 1) * side])
            row_lhs[i * local + j] = jnp.concatenate([high, low], axis=0)

    def second(step, carry):
        blank = jnp.zeros((2 * vecs, side), BF16)
        for u in range(UNROLL):
            pair = step * UNROLL + u
            one = row_lhs[rows_s[0, 2 * pair]]
            two = row_lhs[rows_s[0, 2 * pair + 1]]
            lhs = jnp.concatenate([
                jnp.concatenate([one, blank], axis=1),
                jnp.concatenate([blank, two], axis=1),
            ], axis=0)
            rhs = both[pl.ds(pl.multiple_of(pair * 2 * side, 2 * side), 2 * side), :]
            got = jnp.dot(lhs, rhs, preferred_element_type=F32)
            got = got[:, 0:side] + got[:, side:]
            place = pl.multiple_of(pair * 2 * vecs, 2 * vecs)
            terms[pl.ds(place, vecs), :] = got[0:vecs] + got[vecs:2 * vecs]
            terms[pl.ds(place + vecs, vecs), :] = got[2 * vecs:3 * vecs] + got[3 * vecs:]
        return carry

    lax.fori_loop(0, slots // (2 * UNROLL), second, 0)
    col_part[...] = add_up(col_hits).reshape(col_blocks, vecs, side)
    colp = []
    for n, peer in enumerate(row_peers):
        colp.append(pltpu.make_async_remote_copy(
            src_ref=col_part.at[pl.ds(peer[0] * local, local)], dst_ref=col_in.at[n],
            send_sem=colp_send.at[n], recv_sem=colp_recv.at[n], device_id=peer, device_id_type=MESH))
        colp[-1].start()

    total = row_part[pl.ds(c * local, local)] + col_part[pl.ds(r * local, local)]
    for n, copy in enumerate(rowp):
        copy.wait()
        total += row_in[n]
    for n, copy in enumerate(colp):
        copy.wait()
        total += col_in[n]
    for j in range(local):
        out_ref[:, j * side:(j + 1) * side] = total[j]


def body(tiles, tile_rows, tile_cols, tile_counts, vectors):
    vecs, width = vectors.shape
    slots, side = tiles.shape[2:4]
    row_devices = lax.axis_size("row")
    column_devices = lax.axis_size("col")
    local = width // side
    row_blocks = column_devices * local
    col_blocks = row_devices * local
    rows = tile_rows.reshape(1, slots)
    cols = tile_cols.reshape(1, slots)
    vmem = pl.BlockSpec(memory_space=pltpu.VMEM)
    dma = pltpu.SemaphoreType.DMA
    return pl.pallas_call(
        kernel,
        out_shape=pltpu.VMEM((vecs, width), F32),
        in_specs=[pl.BlockSpec(memory_space=pltpu.HBM)] * 5,
        out_specs=vmem,
        scratch_shapes=[
            pltpu.SMEM((1, slots), jnp.int32),
            pltpu.SMEM((1, slots), jnp.int32),
            pltpu.SMEM((1, 1), jnp.int32),
            pltpu.VMEM((1, slots), jnp.int32),
            pltpu.VMEM((1, slots), jnp.int32),
            pltpu.VMEM((slots, side, side), F32),
            pltpu.VMEM((slots * side, 2 * side), BF16),
            pltpu.VMEM((row_devices, vecs, width), F32),
            pltpu.VMEM((column_devices, vecs, width), F32),
            pltpu.VMEM((col_blocks, 2 * vecs, 2 * side), BF16),
            pltpu.VMEM((row_blocks, 2 * vecs, side), BF16),
            pltpu.VMEM((row_blocks * vecs, slots * vecs), BF16),
            pltpu.VMEM((col_blocks * vecs, slots * vecs), BF16),
            pltpu.VMEM((slots * vecs, side), F32),
            pltpu.VMEM((row_blocks, vecs, side), F32),
            pltpu.VMEM((col_blocks, vecs, side), F32),
            pltpu.VMEM((column_devices - 1, local, vecs, side), F32),
            pltpu.VMEM((row_devices - 1, local, vecs, side), F32),
            dma((7,)),
            dma((CHUNKS,)),
            dma((row_devices - 1,)),
            dma((row_devices - 1,)),
            dma((column_devices - 1,)),
            dma((column_devices - 1,)),
            dma((column_devices - 1,)),
            dma((column_devices - 1,)),
            dma((row_devices - 1,)),
            dma((row_devices - 1,)),
        ],
        compiler_params=pltpu.CompilerParams(
            collective_id=0, has_side_effects=True, vmem_limit_bytes=56 * 2**20
        ),
        cost_estimate=pl.CostEstimate(
            flops=12 * slots * side * side * vecs, bytes_accessed=4 * slots * side * side, transcendentals=0
        ),
        name="symmetric_product",
    )(rows, cols, tile_counts, vectors, tiles.reshape(slots, side, side))


def solution(mesh):
    in_specs = (
        P("row", "col", None, None, None),
        P("row", "col", None),
        P("row", "col", None),
        P("row", "col"),
        P(None, ("row", "col")),
    )
    out_specs = P(None, ("row", "col"))
    return jax.shard_map(body, mesh=mesh, in_specs=in_specs, out_specs=out_specs, check_vma=False)
```

```python
import functools

import jax
import jax.numpy as jnp
from jax import lax
from jax.experimental import pallas as pl
from jax.experimental.pallas import tpu as pltpu
from jax.sharding import PartitionSpec as P

MESH = pl.DeviceIdType.MESH
F32 = jnp.float32
BF16 = jnp.bfloat16
CHUNKS = 8
GROUP = 4
UNROLL = 8


def split(value):
    high = value.astype(BF16)
    low = (value - high.astype(F32)).astype(BF16)
    return high, low


def hit_matrix(labels, count, blocks, vecs):
    slots = labels.shape[1]
    slot = lax.broadcasted_iota(jnp.int32, (vecs, slots), 1)
    names = jnp.where(slot < count, jnp.broadcast_to(labels, (vecs, slots)), -1)
    source = lax.broadcasted_iota(jnp.int32, (slots, slots * vecs), 0)
    target = lax.broadcasted_iota(jnp.int32, (slots, slots * vecs), 1)
    spread = jnp.where((target >= source * vecs) & (target < source * vecs + vecs), 1.0, 0.0).astype(BF16)
    wide = jnp.dot(names.astype(F32).astype(BF16), spread, preferred_element_type=F32)[0:1]
    lane = lax.rem(lax.broadcasted_iota(jnp.int32, (1, slots * vecs), 1), vecs)
    code = wide.astype(jnp.int32) * vecs + lane
    place = lax.broadcasted_iota(jnp.int32, (blocks * vecs, slots * vecs), 0)
    return jnp.where(place == code, 1.0, 0.0).astype(BF16)


def kernel(
    rows_ref, cols_ref, count_ref, x_ref, tiles_ref, out_ref,
    rows_s, cols_s, count_s, rows_v, cols_v, raw, both, col_x, row_x, col_lhs, row_lhs, row_hits, col_hits, terms, row_part, col_part, row_in, col_in,
    small_sem, tile_sem, colx_send, colx_recv, rowx_send, rowx_recv, rowp_send, rowp_recv, colp_send, colp_recv,
):
    row_devices = lax.axis_size("row")
    column_devices = lax.axis_size("col")
    r = lax.axis_index("row")
    c = lax.axis_index("col")
    vecs, width = x_ref.shape
    slots, side, _ = tiles_ref.shape
    local = width // side
    row_blocks = column_devices * local
    col_blocks = row_devices * local
    chunk = slots // CHUNKS

    row_peers = [(lax.rem(r + d, row_devices), c) for d in range(1, row_devices)]
    col_peers = [(r, lax.rem(c + d, column_devices)) for d in range(1, column_devices)]

    barrier = pltpu.get_barrier_semaphore()
    for peer in row_peers + col_peers:
        pl.semaphore_signal(barrier, inc=1, device_id=peer, device_id_type=MESH)

    smalls = [
        pltpu.make_async_copy(source, target, small_sem.at[n])
        for n, (source, target) in enumerate([
            (rows_ref, rows_v), (cols_ref, cols_v), (count_ref, count_s), (rows_ref, rows_s), (cols_ref, cols_s),
            (x_ref, col_x.at[r]), (x_ref, row_x.at[c]),
        ])
    ]
    for copy in smalls:
        copy.start()
    fetches = []
    for n in range(CHUNKS):
        piece = pl.ds(n * chunk, chunk)
        fetch = pltpu.make_async_copy(tiles_ref.at[piece], raw.at[piece], tile_sem.at[n])
        fetch.start()
        fetches.append(fetch)
    pl.semaphore_wait(barrier, len(row_peers) + len(col_peers))

    colx, rowx = [], []
    for n, peer in enumerate(row_peers):
        colx.append(pltpu.make_async_remote_copy(
            src_ref=x_ref, dst_ref=col_x.at[r], send_sem=colx_send.at[n], recv_sem=colx_recv.at[n],
            device_id=peer, device_id_type=MESH))
        colx[-1].start()
    for n, peer in enumerate(col_peers):
        rowx.append(pltpu.make_async_remote_copy(
            src_ref=x_ref, dst_ref=row_x.at[c], send_sem=rowx_send.at[n], recv_sem=rowx_recv.at[n],
            device_id=peer, device_id_type=MESH))
        rowx[-1].start()
    for copy in smalls:
        copy.wait()
    count = count_s[0, 0]
    row_hits[...] = hit_matrix(rows_v[...], count, row_blocks, vecs)
    col_hits[...] = hit_matrix(cols_v[...], count, col_blocks, vecs)

    for n in range(CHUNKS):
        fetches[n].wait()

        def halve(t, carry):
            high, low = split(raw[t])
            place = pl.ds(pl.multiple_of(t * side, side), side)
            both[place, 0:side] = high
            both[place, side:] = low
            return carry

        lax.fori_loop(n * chunk, (n + 1) * chunk, halve, 0, unroll=8)

    for copy in colx:
        copy.wait()
    for i in range(row_devices):
        for j in range(local):
            high, low = split(col_x[i, :, j * side:(j + 1) * side])
            n = i * local + j
            upper = jnp.concatenate([high, low], axis=0)
            under = jnp.concatenate([high, jnp.zeros_like(low)], axis=0)
            col_lhs[n, :, 0:side] = upper
            col_lhs[n, :, side:] = under

    def add_up(hits):
        high, low = split(terms[...])
        total = jnp.dot(hits[...], jnp.concatenate([high, low], axis=1), preferred_element_type=F32)
        return total[:, 0:side] + total[:, side:]

    def first(step, carry):
        for u in range(UNROLL):
            quad = step * UNROLL + u
            lhs = jnp.concatenate([col_lhs[cols_s[0, GROUP * quad + q]] for q in range(GROUP)], axis=0)
            rhs = both[pl.ds(pl.multiple_of(quad * GROUP * side, GROUP * side), GROUP * side), :]
            got = lax.dot_general(lhs, rhs, (((1,), (1,)), ((), ())), preferred_element_type=F32)
            place = pl.multiple_of(quad * GROUP * vecs, GROUP * vecs)
            for q in range(GROUP):
                own = got[2 * q * vecs:2 * (q + 1) * vecs, q * side:(q + 1) * side]
                terms[pl.ds(place + q * vecs, vecs), :] = own[0:vecs] + own[vecs:]
        return carry

    lax.fori_loop(0, slots // (GROUP * UNROLL), first, 0)
    row_part[...] = add_up(row_hits).reshape(row_blocks, vecs, side)
    rowp = []
    for n, peer in enumerate(col_peers):
        rowp.append(pltpu.make_async_remote_copy(
            src_ref=row_part.at[pl.ds(peer[1] * local, local)], dst_ref=row_in.at[n],
            send_sem=rowp_send.at[n], recv_sem=rowp_recv.at[n], device_id=peer, device_id_type=MESH))
        rowp[-1].start()

    for copy in rowx:
        copy.wait()
    for i in range(column_devices):
        for j in range(local):
            high, low = split(row_x[i, :, j * side:(j + 1) * side])
            row_lhs[i * local + j] = jnp.concatenate([high, low], axis=0)

    def second(step, carry):
        blank = jnp.zeros((2 * vecs, side), BF16)
        for u in range(UNROLL):
            quad = step * UNROLL + u
            parts = [row_lhs[rows_s[0, GROUP * quad + q]] for q in range(GROUP)]
            lhs = jnp.concatenate([
                jnp.concatenate([part, blank] if q % 2 == 0 else [blank, part], axis=1)
                for q, part in enumerate(parts)
            ], axis=0)
            start = pl.multiple_of(quad * GROUP * side, GROUP * side)
            rhs = jnp.concatenate([
                both[pl.ds(start + 2 * h * side, 2 * side), :] for h in range(GROUP // 2)
            ], axis=1)
            got = jnp.dot(lhs, rhs, preferred_element_type=F32)
            place = pl.multiple_of(quad * GROUP * vecs, GROUP * vecs)
            for q in range(GROUP):
                h = q // 2
                own = got[2 * q * vecs:2 * (q + 1) * vecs, 2 * h * side:2 * (h + 1) * side]
                own = own[0:vecs] + own[vecs:]
                terms[pl.ds(place + q * vecs, vecs), :] = own[:, 0:side] + own[:, side:]
        return carry

    lax.fori_loop(0, slots // (GROUP * UNROLL), second, 0)
    col_part[...] = add_up(col_hits).reshape(col_blocks, vecs, side)
    colp = []
    for n, peer in enumerate(row_peers):
        colp.append(pltpu.make_async_remote_copy(
            src_ref=col_part.at[pl.ds(peer[0] * local, local)], dst_ref=col_in.at[n],
            send_sem=colp_send.at[n], recv_sem=colp_recv.at[n], device_id=peer, device_id_type=MESH))
        colp[-1].start()

    total = row_part[pl.ds(c * local, local)] + col_part[pl.ds(r * local, local)]
    for n, copy in enumerate(rowp):
        copy.wait()
        total += row_in[n]
    for n, copy in enumerate(colp):
        copy.wait()
        total += col_in[n]
    for j in range(local):
        out_ref[:, j * side:(j + 1) * side] = total[j]


def body(tiles, tile_rows, tile_cols, tile_counts, vectors):
    vecs, width = vectors.shape
    slots, side = tiles.shape[2:4]
    row_devices = lax.axis_size("row")
    column_devices = lax.axis_size("col")
    local = width // side
    row_blocks = column_devices * local
    col_blocks = row_devices * local
    rows = tile_rows.reshape(1, slots)
    cols = tile_cols.reshape(1, slots)
    vmem = pl.BlockSpec(memory_space=pltpu.VMEM)
    dma = pltpu.SemaphoreType.DMA
    return pl.pallas_call(
        kernel,
        out_shape=pltpu.VMEM((vecs, width), F32),
        in_specs=[pl.BlockSpec(memory_space=pltpu.HBM)] * 5,
        out_specs=vmem,
        scratch_shapes=[
            pltpu.SMEM((1, slots), jnp.int32),
            pltpu.SMEM((1, slots), jnp.int32),
            pltpu.SMEM((1, 1), jnp.int32),
            pltpu.VMEM((1, slots), jnp.int32),
            pltpu.VMEM((1, slots), jnp.int32),
            pltpu.VMEM((slots, side, side), F32),
            pltpu.VMEM((slots * side, 2 * side), BF16),
            pltpu.VMEM((row_devices, vecs, width), F32),
            pltpu.VMEM((column_devices, vecs, width), F32),
            pltpu.VMEM((col_blocks, 2 * vecs, 2 * side), BF16),
            pltpu.VMEM((row_blocks, 2 * vecs, side), BF16),
            pltpu.VMEM((row_blocks * vecs, slots * vecs), BF16),
            pltpu.VMEM((col_blocks * vecs, slots * vecs), BF16),
            pltpu.VMEM((slots * vecs, side), F32),
            pltpu.VMEM((row_blocks, vecs, side), F32),
            pltpu.VMEM((col_blocks, vecs, side), F32),
            pltpu.VMEM((column_devices - 1, local, vecs, side), F32),
            pltpu.VMEM((row_devices - 1, local, vecs, side), F32),
            dma((7,)),
            dma((CHUNKS,)),
            dma((row_devices - 1,)),
            dma((row_devices - 1,)),
            dma((column_devices - 1,)),
            dma((column_devices - 1,)),
            dma((column_devices - 1,)),
            dma((column_devices - 1,)),
            dma((row_devices - 1,)),
            dma((row_devices - 1,)),
        ],
        compiler_params=pltpu.CompilerParams(
            collective_id=0, has_side_effects=True, vmem_limit_bytes=56 * 2**20
        ),
        cost_estimate=pl.CostEstimate(
            flops=12 * slots * side * side * vecs, bytes_accessed=4 * slots * side * side, transcendentals=0
        ),
        name="symmetric_product",
    )(rows, cols, tile_counts, vectors, tiles.reshape(slots, side, side))


def solution(mesh):
    in_specs = (
        P("row", "col", None, None, None),
        P("row", "col", None),
        P("row", "col", None),
        P("row", "col"),
        P(None, ("row", "col")),
    )
    out_specs = P(None, ("row", "col"))
    return jax.shard_map(body, mesh=mesh, in_specs=in_specs, out_specs=out_specs, check_vma=False)
```

```python
import functools

import jax
import jax.numpy as jnp
from jax import lax
from jax.experimental import pallas as pl
from jax.experimental.pallas import tpu as pltpu
from jax.sharding import PartitionSpec as P

MESH = pl.DeviceIdType.MESH
F32 = jnp.float32
BF16 = jnp.bfloat16
CHUNKS = 8
GROUP = 2
UNROLL = 16


def split(value):
    high = value.astype(BF16)
    low = (value - high.astype(F32)).astype(BF16)
    return high, low


def hit_matrix(labels, count, blocks):
    slots = labels.shape[1]
    slot = lax.broadcasted_iota(jnp.int32, (blocks, slots), 1)
    block = lax.broadcasted_iota(jnp.int32, (blocks, slots), 0)
    hits = jnp.where((slot < count) & (block == jnp.broadcast_to(labels, (blocks, slots))), 1.0, 0.0).astype(BF16)
    return jnp.concatenate([hits, hits], axis=1)


def kernel(
    rows_ref, cols_ref, count_ref, x_ref, tiles_ref, out_ref,
    rows_s, cols_s, count_s, rows_v, cols_v, raw, both, col_x, row_x, col_lhs, row_lhs, terms, row_part, col_part, row_in, col_in,
    small_sem, tile_sem, colx_send, colx_recv, rowx_send, rowx_recv, rowp_send, rowp_recv, colp_send, colp_recv,
):
    row_devices = lax.axis_size("row")
    column_devices = lax.axis_size("col")
    r = lax.axis_index("row")
    c = lax.axis_index("col")
    vecs, width = x_ref.shape
    slots, side, _ = tiles_ref.shape
    local = width // side
    row_blocks = column_devices * local
    col_blocks = row_devices * local
    chunk = slots // CHUNKS
    stride = GROUP * UNROLL
    span = local * vecs
    most = (slots * (r + 1) + row_devices - 1) // row_devices
    steps = (most + stride - 1) // stride
    chunks = steps * (stride // chunk)

    row_peers = [(lax.rem(r + d, row_devices), c) for d in range(1, row_devices)]
    col_peers = [(r, lax.rem(c + d, column_devices)) for d in range(1, column_devices)]

    barrier = pltpu.get_barrier_semaphore()
    for peer in row_peers + col_peers:
        pl.semaphore_signal(barrier, inc=1, device_id=peer, device_id_type=MESH)

    smalls = [
        pltpu.make_async_copy(source, target, small_sem.at[n])
        for n, (source, target) in enumerate([
            (rows_ref, rows_v), (cols_ref, cols_v), (count_ref, count_s), (rows_ref, rows_s), (cols_ref, cols_s),
            (x_ref, col_x.at[r]), (x_ref, row_x.at[c]),
        ])
    ]
    for copy in smalls:
        copy.start()

    def fetch(n):
        piece = pl.ds(n * chunk, chunk)
        return pltpu.make_async_copy(tiles_ref.at[piece], raw.at[piece], tile_sem.at[n])

    def begin(n, carry):
        fetch(n).start()
        return carry

    lax.fori_loop(0, chunks, begin, 0)
    pl.semaphore_wait(barrier, len(row_peers) + len(col_peers))

    colx, rowx = [], []
    for n, peer in enumerate(row_peers):
        colx.append(pltpu.make_async_remote_copy(
            src_ref=x_ref, dst_ref=col_x.at[r], send_sem=colx_send.at[n], recv_sem=colx_recv.at[n],
            device_id=peer, device_id_type=MESH))
        colx[-1].start()
    for n, peer in enumerate(col_peers):
        rowx.append(pltpu.make_async_remote_copy(
            src_ref=x_ref, dst_ref=row_x.at[c], send_sem=rowx_send.at[n], recv_sem=rowx_recv.at[n],
            device_id=peer, device_id_type=MESH))
        rowx[-1].start()
    for copy in smalls:
        copy.wait()
    terms[...] = jnp.zeros_like(terms)

    def halve(n, carry):
        fetch(n).wait()

        def one(i, carry):
            t = n * chunk + i
            high, low = split(raw[t])
            place = pl.ds(pl.multiple_of(t * side, side), side)
            both[place, 0:side] = high
            both[place, side:] = low
            return carry

        return lax.fori_loop(0, chunk, one, carry, unroll=8)

    lax.fori_loop(0, chunks, halve, 0)

    count = count_s[0, 0]
    row_hits = hit_matrix(rows_v[...], count, row_blocks)
    col_hits = hit_matrix(cols_v[...], count, col_blocks)

    for copy in colx:
        copy.wait()
    for i in range(row_devices):
        for j in range(local):
            high, low = split(col_x[i, :, j * side:(j + 1) * side])
            n = i * local + j
            upper = jnp.concatenate([high, low], axis=0)
            under = jnp.concatenate([high, jnp.zeros_like(low)], axis=0)
            col_lhs[n, :, 0:side] = upper
            col_lhs[n, :, side:] = under

    def add_up(hits, part):
        blocks = hits.shape[0]
        for k in range(0, vecs, 2):
            halves = [split(terms[pl.ds(k + m, slots, stride=vecs), :]) for m in range(2)]
            stacked = jnp.concatenate([jnp.concatenate(half, axis=0) for half in halves], axis=1)
            total = jnp.dot(hits, stacked, preferred_element_type=F32)
            for m in range(2):
                part[pl.ds(k + m, blocks, stride=vecs), :] = total[:, m * side:(m + 1) * side]

    def first(step, carry):
        for u in range(UNROLL):
            quad = step * UNROLL + u
            lhs = jnp.concatenate([col_lhs[cols_s[0, GROUP * quad + q]] for q in range(GROUP)], axis=0)
            rhs = both[pl.ds(pl.multiple_of(quad * GROUP * side, GROUP * side), GROUP * side), :]
            got = lax.dot_general(lhs, rhs, (((1,), (1,)), ((), ())), preferred_element_type=F32)
            place = pl.multiple_of(quad * GROUP * vecs, GROUP * vecs)
            for q in range(GROUP):
                own = got[2 * q * vecs:2 * (q + 1) * vecs, q * side:(q + 1) * side]
                terms[pl.ds(place + q * vecs, vecs), :] = own[0:vecs] + own[vecs:]
        return carry

    lax.fori_loop(0, steps, first, 0)
    add_up(row_hits, row_part)
    rowp = []
    for n, peer in enumerate(col_peers):
        rowp.append(pltpu.make_async_remote_copy(
            src_ref=row_part.at[pl.ds(pl.multiple_of(peer[1] * span, span), span)], dst_ref=row_in.at[n],
            send_sem=rowp_send.at[n], recv_sem=rowp_recv.at[n], device_id=peer, device_id_type=MESH))
        rowp[-1].start()

    for copy in rowx:
        copy.wait()
    for i in range(column_devices):
        for j in range(local):
            high, low = split(row_x[i, :, j * side:(j + 1) * side])
            row_lhs[i * local + j] = jnp.concatenate([high, low], axis=0)

    def second(step, carry):
        blank = jnp.zeros((2 * vecs, side), BF16)
        for u in range(UNROLL):
            quad = step * UNROLL + u
            parts = [row_lhs[rows_s[0, GROUP * quad + q]] for q in range(GROUP)]
            lhs = jnp.concatenate([
                jnp.concatenate([part, blank] if q % 2 == 0 else [blank, part], axis=1)
                for q, part in enumerate(parts)
            ], axis=0)
            start = pl.multiple_of(quad * GROUP * side, GROUP * side)
            rhs = jnp.concatenate([
                both[pl.ds(start + 2 * h * side, 2 * side), :] for h in range(GROUP // 2)
            ], axis=1)
            got = jnp.dot(lhs, rhs, preferred_element_type=F32)
            place = pl.multiple_of(quad * GROUP * vecs, GROUP * vecs)
            for q in range(GROUP):
                h = q // 2
                own = got[2 * q * vecs:2 * (q + 1) * vecs, 2 * h * side:2 * (h + 1) * side]
                own = own[0:vecs] + own[vecs:]
                terms[pl.ds(place + q * vecs, vecs), :] = own[:, 0:side] + own[:, side:]
        return carry

    lax.fori_loop(0, steps, second, 0)
    add_up(col_hits, col_part)
    colp = []
    for n, peer in enumerate(row_peers):
        colp.append(pltpu.make_async_remote_copy(
            src_ref=col_part.at[pl.ds(pl.multiple_of(peer[0] * span, span), span)], dst_ref=col_in.at[n],
            send_sem=colp_send.at[n], recv_sem=colp_recv.at[n], device_id=peer, device_id_type=MESH))
        colp[-1].start()

    total = row_part[pl.ds(pl.multiple_of(c * span, span), span)] + col_part[pl.ds(pl.multiple_of(r * span, span), span)]
    for n, copy in enumerate(rowp):
        copy.wait()
        total += row_in[n]
    for n, copy in enumerate(colp):
        copy.wait()
        total += col_in[n]
    for j in range(local):
        out_ref[:, j * side:(j + 1) * side] = total[j * vecs:(j + 1) * vecs]


def body(tiles, tile_rows, tile_cols, tile_counts, vectors):
    vecs, width = vectors.shape
    slots, side = tiles.shape[2:4]
    row_devices = lax.axis_size("row")
    column_devices = lax.axis_size("col")
    local = width // side
    row_blocks = column_devices * local
    col_blocks = row_devices * local
    rows = tile_rows.reshape(1, slots)
    cols = tile_cols.reshape(1, slots)
    vmem = pl.BlockSpec(memory_space=pltpu.VMEM)
    dma = pltpu.SemaphoreType.DMA
    return pl.pallas_call(
        kernel,
        out_shape=pltpu.VMEM((vecs, width), F32),
        in_specs=[pl.BlockSpec(memory_space=pltpu.HBM)] * 5,
        out_specs=vmem,
        scratch_shapes=[
            pltpu.SMEM((1, slots), jnp.int32),
            pltpu.SMEM((1, slots), jnp.int32),
            pltpu.SMEM((1, 1), jnp.int32),
            pltpu.VMEM((1, slots), jnp.int32),
            pltpu.VMEM((1, slots), jnp.int32),
            pltpu.VMEM((slots, side, side), F32),
            pltpu.VMEM((slots * side, 2 * side), BF16),
            pltpu.VMEM((row_devices, vecs, width), F32),
            pltpu.VMEM((column_devices, vecs, width), F32),
            pltpu.VMEM((col_blocks, 2 * vecs, 2 * side), BF16),
            pltpu.VMEM((row_blocks, 2 * vecs, side), BF16),
            pltpu.VMEM((slots * vecs, side), F32),
            pltpu.VMEM((row_blocks * vecs, side), F32),
            pltpu.VMEM((col_blocks * vecs, side), F32),
            pltpu.VMEM((column_devices - 1, local * vecs, side), F32),
            pltpu.VMEM((row_devices - 1, local * vecs, side), F32),
            dma((7,)),
            dma((CHUNKS,)),
            dma((row_devices - 1,)),
            dma((row_devices - 1,)),
            dma((column_devices - 1,)),
            dma((column_devices - 1,)),
            dma((column_devices - 1,)),
            dma((column_devices - 1,)),
            dma((row_devices - 1,)),
            dma((row_devices - 1,)),
        ],
        compiler_params=pltpu.CompilerParams(
            collective_id=0, has_side_effects=True, vmem_limit_bytes=56 * 2**20
        ),
        cost_estimate=pl.CostEstimate(
            flops=12 * slots * side * side * vecs, bytes_accessed=4 * slots * side * side, transcendentals=0
        ),
        name="symmetric_product",
    )(rows, cols, tile_counts, vectors, tiles.reshape(slots, side, side))


def solution(mesh):
    in_specs = (
        P("row", "col", None, None, None),
        P("row", "col", None),
        P("row", "col", None),
        P("row", "col"),
        P(None, ("row", "col")),
    )
    out_specs = P(None, ("row", "col"))
    return jax.shard_map(body, mesh=mesh, in_specs=in_specs, out_specs=out_specs, check_vma=False)
```

```python
import functools

import jax
import jax.numpy as jnp
from jax import lax
from jax.experimental import pallas as pl
from jax.experimental.pallas import tpu as pltpu
from jax.sharding import PartitionSpec as P

MESH = pl.DeviceIdType.MESH
F32 = jnp.float32
BF16 = jnp.bfloat16
CHUNKS = 8
GROUP = 2
UNROLL = 16
AHEAD = 2


def split(value):
    high = value.astype(BF16)
    low = (value - high.astype(F32)).astype(BF16)
    return high, low


def stack(value):
    high = value.astype(BF16).astype(F32)
    return jnp.concatenate([high, value - high], axis=0).astype(BF16)


def hit_matrix(labels, count, blocks):
    slots = labels.shape[1]
    slot = lax.broadcasted_iota(jnp.int32, (blocks, slots), 1)
    block = lax.broadcasted_iota(jnp.int32, (blocks, slots), 0)
    hits = jnp.where((slot < count) & (block == jnp.broadcast_to(labels, (blocks, slots))), 1.0, 0.0).astype(BF16)
    return jnp.concatenate([hits, hits], axis=1)


def kernel(
    rows_ref, cols_ref, count_ref, x_ref, tiles_ref, out_ref,
    rows_s, cols_s, count_s, rows_v, cols_v, raw, both, col_x, row_x, col_lhs, row_lhs, row_terms, col_terms, row_part, col_part, row_in, col_in,
    small_sem, tile_sem, colx_send, colx_recv, rowx_send, rowx_recv, rowp_send, rowp_recv, colp_send, colp_recv,
):
    row_devices = lax.axis_size("row")
    column_devices = lax.axis_size("col")
    r = lax.axis_index("row")
    c = lax.axis_index("col")
    vecs, width = x_ref.shape
    slots, side, _ = tiles_ref.shape
    local = width // side
    row_blocks = column_devices * local
    col_blocks = row_devices * local
    chunk = slots // CHUNKS
    stride = GROUP * UNROLL
    span = local * vecs
    most = (slots * (r + 1) + row_devices - 1) // row_devices
    steps = (most + stride - 1) // stride
    chunks = steps * (stride // chunk)

    row_peers = [(lax.rem(r + d, row_devices), c) for d in range(1, row_devices)]
    col_peers = [(r, lax.rem(c + d, column_devices)) for d in range(1, column_devices)]

    barrier = pltpu.get_barrier_semaphore()
    for peer in row_peers + col_peers:
        pl.semaphore_signal(barrier, inc=1, device_id=peer, device_id_type=MESH)

    smalls = [
        pltpu.make_async_copy(source, target, small_sem.at[n])
        for n, (source, target) in enumerate([
            (rows_ref, rows_v), (cols_ref, cols_v), (count_ref, count_s), (rows_ref, rows_s), (cols_ref, cols_s),
            (x_ref, col_x.at[r]), (x_ref, row_x.at[c]),
        ])
    ]
    for copy in smalls:
        copy.start()

    def fetch(n):
        piece = pl.ds(n * chunk, chunk)
        return pltpu.make_async_copy(tiles_ref.at[piece], raw.at[piece], tile_sem.at[n])

    def begin(n, carry):
        fetch(n).start()
        return carry

    lax.fori_loop(0, chunks, begin, 0)
    pl.semaphore_wait(barrier, len(row_peers) + len(col_peers))

    colx, rowx = [], []
    for n, peer in enumerate(row_peers):
        colx.append(pltpu.make_async_remote_copy(
            src_ref=x_ref, dst_ref=col_x.at[r], send_sem=colx_send.at[n], recv_sem=colx_recv.at[n],
            device_id=peer, device_id_type=MESH))
        colx[-1].start()
    for n, peer in enumerate(col_peers):
        rowx.append(pltpu.make_async_remote_copy(
            src_ref=x_ref, dst_ref=row_x.at[c], send_sem=rowx_send.at[n], recv_sem=rowx_recv.at[n],
            device_id=peer, device_id_type=MESH))
        rowx[-1].start()
    for copy in smalls:
        copy.wait()
    row_terms[...] = jnp.zeros_like(row_terms)
    col_terms[...] = jnp.zeros_like(col_terms)

    def halve(n, carry):
        fetch(n).wait()

        def one(i, carry):
            t = n * chunk + i
            high, low = split(raw[t])
            place = pl.ds(pl.multiple_of(t * side, side), side)
            both[place, 0:side] = high
            both[place, side:] = low
            return carry

        return lax.fori_loop(0, chunk, one, carry, unroll=8)

    lax.fori_loop(0, chunks, halve, 0)

    count = count_s[0, 0]
    row_hits = hit_matrix(rows_v[...], count, row_blocks)
    col_hits = hit_matrix(cols_v[...], count, col_blocks)

    for copy in colx:
        copy.wait()
    for i in range(row_devices):
        for j in range(local):
            n = i * local + j
            piece = stack(col_x[i, :, j * side:(j + 1) * side])
            col_lhs[n, :, 0:side] = piece
            col_lhs[n, :, side:] = piece

    def add_up(hits, terms, part):
        blocks = hits.shape[0]
        for k in range(0, vecs, 2):
            halves = [split(terms[pl.ds(k + m, slots, stride=vecs), :]) for m in range(2)]
            stacked = jnp.concatenate([jnp.concatenate(half, axis=0) for half in halves], axis=1)
            total = jnp.dot(hits, stacked, preferred_element_type=F32)
            for m in range(2):
                part[pl.ds(k + m, blocks, stride=vecs), :] = total[:, m * side:(m + 1) * side]

    def first(step, carry):
        for u in range(UNROLL):
            quad = step * UNROLL + u
            lhs = jnp.concatenate([col_lhs[cols_s[0, GROUP * quad + q]] for q in range(GROUP)], axis=0)
            rhs = both[pl.ds(pl.multiple_of(quad * GROUP * side, GROUP * side), GROUP * side), :]
            got = lax.dot_general(lhs, rhs, (((1,), (1,)), ((), ())), preferred_element_type=F32)
            place = pl.multiple_of(quad * GROUP * vecs, GROUP * vecs)
            for q in range(GROUP):
                own = got[2 * q * vecs:2 * (q + 1) * vecs, q * side:(q + 1) * side]
                row_terms[pl.ds(place + q * vecs, vecs), :] = own[0:vecs] + own[vecs:]
        return carry

    rowp = []
    for n, peer in enumerate(col_peers):
        rowp.append(pltpu.make_async_remote_copy(
            src_ref=row_part.at[pl.ds(pl.multiple_of(peer[1] * span, span), span)], dst_ref=row_in.at[n],
            send_sem=rowp_send.at[n], recv_sem=rowp_recv.at[n], device_id=peer, device_id_type=MESH))

    def finish_rows():
        add_up(row_hits, row_terms, row_part)
        for copy in rowp:
            copy.start()

    late = 2 * r >= row_devices
    ahead = jnp.where(late, jnp.minimum(steps, AHEAD), steps)
    lax.fori_loop(0, ahead, first, 0)
    pl.when(jnp.logical_not(late))(finish_rows)

    for copy in rowx:
        copy.wait()
    for i in range(column_devices):
        for j in range(local):
            row_lhs[i * local + j] = stack(row_x[i, :, j * side:(j + 1) * side])

    def second(step, carry):
        blank = jnp.zeros((2 * vecs, side), BF16)
        for u in range(UNROLL):
            quad = step * UNROLL + u
            parts = [row_lhs[rows_s[0, GROUP * quad + q]] for q in range(GROUP)]
            lhs = jnp.concatenate([
                jnp.concatenate([part, blank] if q % 2 == 0 else [blank, part], axis=1)
                for q, part in enumerate(parts)
            ], axis=0)
            start = pl.multiple_of(quad * GROUP * side, GROUP * side)
            rhs = jnp.concatenate([
                both[pl.ds(start + 2 * h * side, 2 * side), :] for h in range(GROUP // 2)
            ], axis=1)
            got = jnp.dot(lhs, rhs, preferred_element_type=F32)
            place = pl.multiple_of(quad * GROUP * vecs, GROUP * vecs)
            for q in range(GROUP):
                h = q // 2
                own = got[2 * q * vecs:2 * (q + 1) * vecs, 2 * h * side:2 * (h + 1) * side]
                own = own[0:vecs] + own[vecs:]
                col_terms[pl.ds(place + q * vecs, vecs), :] = own[:, 0:side] + own[:, side:]
        return carry

    lax.fori_loop(0, steps, second, 0)
    add_up(col_hits, col_terms, col_part)
    colp = []
    for n, peer in enumerate(row_peers):
        colp.append(pltpu.make_async_remote_copy(
            src_ref=col_part.at[pl.ds(pl.multiple_of(peer[0] * span, span), span)], dst_ref=col_in.at[n],
            send_sem=colp_send.at[n], recv_sem=colp_recv.at[n], device_id=peer, device_id_type=MESH))
        colp[-1].start()

    lax.fori_loop(ahead, steps, first, 0)
    pl.when(late)(finish_rows)

    total = row_part[pl.ds(pl.multiple_of(c * span, span), span)] + col_part[pl.ds(pl.multiple_of(r * span, span), span)]
    for n, copy in enumerate(rowp):
        copy.wait()
        total += row_in[n]
    for n, copy in enumerate(colp):
        copy.wait()
        total += col_in[n]
    for j in range(local):
        out_ref[:, j * side:(j + 1) * side] = total[j * vecs:(j + 1) * vecs]


def body(tiles, tile_rows, tile_cols, tile_counts, vectors):
    vecs, width = vectors.shape
    slots, side = tiles.shape[2:4]
    row_devices = lax.axis_size("row")
    column_devices = lax.axis_size("col")
    local = width // side
    row_blocks = column_devices * local
    col_blocks = row_devices * local
    rows = tile_rows.reshape(1, slots)
    cols = tile_cols.reshape(1, slots)
    vmem = pl.BlockSpec(memory_space=pltpu.VMEM)
    dma = pltpu.SemaphoreType.DMA
    return pl.pallas_call(
        kernel,
        out_shape=pltpu.VMEM((vecs, width), F32),
        in_specs=[pl.BlockSpec(memory_space=pltpu.HBM)] * 5,
        out_specs=vmem,
        scratch_shapes=[
            pltpu.SMEM((1, slots), jnp.int32),
            pltpu.SMEM((1, slots), jnp.int32),
            pltpu.SMEM((1, 1), jnp.int32),
            pltpu.VMEM((1, slots), jnp.int32),
            pltpu.VMEM((1, slots), jnp.int32),
            pltpu.VMEM((slots, side, side), F32),
            pltpu.VMEM((slots * side, 2 * side), BF16),
            pltpu.VMEM((row_devices, vecs, width), F32),
            pltpu.VMEM((column_devices, vecs, width), F32),
            pltpu.VMEM((col_blocks, 2 * vecs, 2 * side), BF16),
            pltpu.VMEM((row_blocks, 2 * vecs, side), BF16),
            pltpu.VMEM((slots * vecs, side), F32),
            pltpu.VMEM((slots * vecs, side), F32),
            pltpu.VMEM((row_blocks * vecs, side), F32),
            pltpu.VMEM((col_blocks * vecs, side), F32),
            pltpu.VMEM((column_devices - 1, local * vecs, side), F32),
            pltpu.VMEM((row_devices - 1, local * vecs, side), F32),
            dma((7,)),
            dma((CHUNKS,)),
            dma((row_devices - 1,)),
            dma((row_devices - 1,)),
            dma((column_devices - 1,)),
            dma((column_devices - 1,)),
            dma((column_devices - 1,)),
            dma((column_devices - 1,)),
            dma((row_devices - 1,)),
            dma((row_devices - 1,)),
        ],
        compiler_params=pltpu.CompilerParams(
            collective_id=0, has_side_effects=True, vmem_limit_bytes=56 * 2**20
        ),
        cost_estimate=pl.CostEstimate(
            flops=12 * slots * side * side * vecs, bytes_accessed=4 * slots * side * side, transcendentals=0
        ),
        name="symmetric_product",
    )(rows, cols, tile_counts, vectors, tiles.reshape(slots, side, side))


def solution(mesh):
    in_specs = (
        P("row", "col", None, None, None),
        P("row", "col", None),
        P("row", "col", None),
        P("row", "col"),
        P(None, ("row", "col")),
    )
    out_specs = P(None, ("row", "col"))
    return jax.shard_map(body, mesh=mesh, in_specs=in_specs, out_specs=out_specs, check_vma=False)
```

```python
import functools

import jax
import jax.numpy as jnp
from jax import lax
from jax.experimental import pallas as pl
from jax.experimental.pallas import tpu as pltpu
from jax.sharding import PartitionSpec as P

MESH = pl.DeviceIdType.MESH
F32 = jnp.float32
BF16 = jnp.bfloat16
CHUNKS = 8
GROUP = 2
UNROLL = 16
AHEAD = 1


def split(value):
    high = value.astype(BF16)
    low = (value - high.astype(F32)).astype(BF16)
    return high, low


def stack(value):
    high = value.astype(BF16).astype(F32)
    return jnp.concatenate([high, value - high], axis=0).astype(BF16)


def hit_matrix(labels, count, blocks):
    slots = labels.shape[1]
    slot = lax.broadcasted_iota(jnp.int32, (blocks, slots), 1)
    block = lax.broadcasted_iota(jnp.int32, (blocks, slots), 0)
    hits = jnp.where((slot < count) & (block == jnp.broadcast_to(labels, (blocks, slots))), 1.0, 0.0).astype(BF16)
    return jnp.concatenate([hits, hits], axis=1)


def kernel(
    rows_ref, cols_ref, count_ref, x_ref, tiles_ref, out_ref,
    rows_s, cols_s, count_s, rows_v, cols_v, raw, both, col_x, row_x, col_lhs, row_lhs, row_terms, col_terms, row_part, col_part, row_in, col_in,
    small_sem, tile_sem, colx_send, colx_recv, rowx_send, rowx_recv, rowp_send, rowp_recv, colp_send, colp_recv,
):
    row_devices = lax.axis_size("row")
    column_devices = lax.axis_size("col")
    r = lax.axis_index("row")
    c = lax.axis_index("col")
    vecs, width = x_ref.shape
    slots, side, _ = tiles_ref.shape
    local = width // side
    row_blocks = column_devices * local
    col_blocks = row_devices * local
    chunk = slots // CHUNKS
    stride = GROUP * UNROLL
    span = local * vecs
    most = (slots * (r + 1) + row_devices - 1) // row_devices
    steps = (most + stride - 1) // stride
    chunks = steps * (stride // chunk)

    row_peers = [(lax.rem(r + d, row_devices), c) for d in range(1, row_devices)]
    col_peers = [(r, lax.rem(c + d, column_devices)) for d in range(1, column_devices)]

    barrier = pltpu.get_barrier_semaphore()
    for peer in row_peers + col_peers:
        pl.semaphore_signal(barrier, inc=1, device_id=peer, device_id_type=MESH)

    smalls = [
        pltpu.make_async_copy(source, target, small_sem.at[n])
        for n, (source, target) in enumerate([
            (rows_ref, rows_v), (cols_ref, cols_v), (count_ref, count_s), (rows_ref, rows_s), (cols_ref, cols_s),
            (x_ref, col_x.at[r]), (x_ref, row_x.at[c]),
        ])
    ]
    for copy in smalls:
        copy.start()

    def fetch(n):
        piece = pl.ds(n * chunk, chunk)
        return pltpu.make_async_copy(tiles_ref.at[piece], raw.at[piece], tile_sem.at[n])

    def begin(n, carry):
        fetch(n).start()
        return carry

    lax.fori_loop(0, chunks, begin, 0)
    pl.semaphore_wait(barrier, len(row_peers) + len(col_peers))

    colx, rowx = [], []
    for n, peer in enumerate(row_peers):
        colx.append(pltpu.make_async_remote_copy(
            src_ref=x_ref, dst_ref=col_x.at[r], send_sem=colx_send.at[n], recv_sem=colx_recv.at[n],
            device_id=peer, device_id_type=MESH))
        colx[-1].start()
    arrivals = []
    for n in range(column_devices - 1):
        other = jnp.where(n < c, n, n + 1)
        rowx.append(pltpu.make_async_remote_copy(
            src_ref=x_ref, dst_ref=row_x.at[c], send_sem=rowx_send.at[n], recv_sem=rowx_recv.at[c],
            device_id=(r, other), device_id_type=MESH))
        rowx[-1].start()
        arrivals.append(pltpu.make_async_remote_copy(
            src_ref=x_ref, dst_ref=row_x.at[other], send_sem=rowx_send.at[n], recv_sem=rowx_recv.at[other],
            device_id=(r, other), device_id_type=MESH))
    for copy in smalls:
        copy.wait()
    row_terms[...] = jnp.zeros_like(row_terms)
    col_terms[...] = jnp.zeros_like(col_terms)

    def halve(n, carry):
        fetch(n).wait()

        def one(i, carry):
            t = n * chunk + i
            high, low = split(raw[t])
            place = pl.ds(pl.multiple_of(t * side, side), side)
            both[place, 0:side] = high
            both[place, side:] = low
            return carry

        return lax.fori_loop(0, chunk, one, carry, unroll=8)

    lax.fori_loop(0, chunks, halve, 0)

    count = count_s[0, 0]
    row_hits = hit_matrix(rows_v[...], count, row_blocks)
    col_hits = hit_matrix(cols_v[...], count, col_blocks)

    for copy in colx:
        copy.wait()
    for i in range(row_devices):
        for j in range(local):
            n = i * local + j
            piece = stack(col_x[i, :, j * side:(j + 1) * side])
            col_lhs[n, :, 0:side] = piece
            col_lhs[n, :, side:] = piece

    def add_up(hits, terms, part):
        blocks = hits.shape[0]
        for k in range(0, vecs, 2):
            halves = [split(terms[pl.ds(k + m, slots, stride=vecs), :]) for m in range(2)]
            stacked = jnp.concatenate([jnp.concatenate(half, axis=0) for half in halves], axis=1)
            total = jnp.dot(hits, stacked, preferred_element_type=F32)
            for m in range(2):
                part[pl.ds(k + m, blocks, stride=vecs), :] = total[:, m * side:(m + 1) * side]

    def first(step, carry):
        for u in range(UNROLL):
            quad = step * UNROLL + u
            lhs = jnp.concatenate([col_lhs[cols_s[0, GROUP * quad + q]] for q in range(GROUP)], axis=0)
            rhs = both[pl.ds(pl.multiple_of(quad * GROUP * side, GROUP * side), GROUP * side), :]
            got = lax.dot_general(lhs, rhs, (((1,), (1,)), ((), ())), preferred_element_type=F32)
            place = pl.multiple_of(quad * GROUP * vecs, GROUP * vecs)
            for q in range(GROUP):
                own = got[2 * q * vecs:2 * (q + 1) * vecs, q * side:(q + 1) * side]
                row_terms[pl.ds(place + q * vecs, vecs), :] = own[0:vecs] + own[vecs:]
        return carry

    rowp = []
    for n, peer in enumerate(col_peers):
        rowp.append(pltpu.make_async_remote_copy(
            src_ref=row_part.at[pl.ds(pl.multiple_of(peer[1] * span, span), span)], dst_ref=row_in.at[n],
            send_sem=rowp_send.at[n], recv_sem=rowp_recv.at[n], device_id=peer, device_id_type=MESH))

    def finish_rows():
        add_up(row_hits, row_terms, row_part)
        for copy in rowp:
            copy.start()

    late = jnp.logical_and(2 * r >= row_devices, c == 0)
    ahead = jnp.where(late, jnp.minimum(steps, AHEAD), steps)
    lax.fori_loop(0, ahead, first, 0)
    pl.when(jnp.logical_not(late))(finish_rows)

    for sent, arrival in zip(rowx, arrivals):
        sent.wait_send()
        arrival.wait_recv()
    for i in range(column_devices):
        for j in range(local):
            row_lhs[i * local + j] = stack(row_x[i, :, j * side:(j + 1) * side])

    def second(step, carry):
        blank = jnp.zeros((2 * vecs, side), BF16)
        for u in range(UNROLL):
            quad = step * UNROLL + u
            parts = [row_lhs[rows_s[0, GROUP * quad + q]] for q in range(GROUP)]
            lhs = jnp.concatenate([
                jnp.concatenate([part, blank] if q % 2 == 0 else [blank, part], axis=1)
                for q, part in enumerate(parts)
            ], axis=0)
            start = pl.multiple_of(quad * GROUP * side, GROUP * side)
            rhs = jnp.concatenate([
                both[pl.ds(start + 2 * h * side, 2 * side), :] for h in range(GROUP // 2)
            ], axis=1)
            got = jnp.dot(lhs, rhs, preferred_element_type=F32)
            place = pl.multiple_of(quad * GROUP * vecs, GROUP * vecs)
            for q in range(GROUP):
                h = q // 2
                own = got[2 * q * vecs:2 * (q + 1) * vecs, 2 * h * side:2 * (h + 1) * side]
                own = own[0:vecs] + own[vecs:]
                col_terms[pl.ds(place + q * vecs, vecs), :] = own[:, 0:side] + own[:, side:]
        return carry

    lax.fori_loop(0, steps, second, 0)
    add_up(col_hits, col_terms, col_part)
    colp = []
    for n, peer in enumerate(row_peers):
        colp.append(pltpu.make_async_remote_copy(
            src_ref=col_part.at[pl.ds(pl.multiple_of(peer[0] * span, span), span)], dst_ref=col_in.at[n],
            send_sem=colp_send.at[n], recv_sem=colp_recv.at[n], device_id=peer, device_id_type=MESH))
        colp[-1].start()

    lax.fori_loop(ahead, steps, first, 0)
    pl.when(late)(finish_rows)

    total = row_part[pl.ds(pl.multiple_of(c * span, span), span)] + col_part[pl.ds(pl.multiple_of(r * span, span), span)]
    for n, copy in enumerate(rowp):
        copy.wait()
        total += row_in[n]
    for n, copy in enumerate(colp):
        copy.wait()
        total += col_in[n]
    for j in range(local):
        out_ref[:, j * side:(j + 1) * side] = total[j * vecs:(j + 1) * vecs]


def body(tiles, tile_rows, tile_cols, tile_counts, vectors):
    vecs, width = vectors.shape
    slots, side = tiles.shape[2:4]
    row_devices = lax.axis_size("row")
    column_devices = lax.axis_size("col")
    local = width // side
    row_blocks = column_devices * local
    col_blocks = row_devices * local
    rows = tile_rows.reshape(1, slots)
    cols = tile_cols.reshape(1, slots)
    vmem = pl.BlockSpec(memory_space=pltpu.VMEM)
    dma = pltpu.SemaphoreType.DMA
    return pl.pallas_call(
        kernel,
        out_shape=pltpu.VMEM((vecs, width), F32),
        in_specs=[pl.BlockSpec(memory_space=pltpu.HBM)] * 5,
        out_specs=vmem,
        scratch_shapes=[
            pltpu.SMEM((1, slots), jnp.int32),
            pltpu.SMEM((1, slots), jnp.int32),
            pltpu.SMEM((1, 1), jnp.int32),
            pltpu.VMEM((1, slots), jnp.int32),
            pltpu.VMEM((1, slots), jnp.int32),
            pltpu.VMEM((slots, side, side), F32),
            pltpu.VMEM((slots * side, 2 * side), BF16),
            pltpu.VMEM((row_devices, vecs, width), F32),
            pltpu.VMEM((column_devices, vecs, width), F32),
            pltpu.VMEM((col_blocks, 2 * vecs, 2 * side), BF16),
            pltpu.VMEM((row_blocks, 2 * vecs, side), BF16),
            pltpu.VMEM((slots * vecs, side), F32),
            pltpu.VMEM((slots * vecs, side), F32),
            pltpu.VMEM((row_blocks * vecs, side), F32),
            pltpu.VMEM((col_blocks * vecs, side), F32),
            pltpu.VMEM((column_devices - 1, local * vecs, side), F32),
            pltpu.VMEM((row_devices - 1, local * vecs, side), F32),
            dma((7,)),
            dma((CHUNKS,)),
            dma((row_devices - 1,)),
            dma((row_devices - 1,)),
            dma((column_devices - 1,)),
            dma((column_devices,)),
            dma((column_devices - 1,)),
            dma((column_devices - 1,)),
            dma((row_devices - 1,)),
            dma((row_devices - 1,)),
        ],
        compiler_params=pltpu.CompilerParams(
            collective_id=0, has_side_effects=True, vmem_limit_bytes=56 * 2**20
        ),
        cost_estimate=pl.CostEstimate(
            flops=12 * slots * side * side * vecs, bytes_accessed=4 * slots * side * side, transcendentals=0
        ),
        name="symmetric_product",
    )(rows, cols, tile_counts, vectors, tiles.reshape(slots, side, side))


def solution(mesh):
    in_specs = (
        P("row", "col", None, None, None),
        P("row", "col", None),
        P("row", "col", None),
        P("row", "col"),
        P(None, ("row", "col")),
    )
    out_specs = P(None, ("row", "col"))
    return jax.shard_map(body, mesh=mesh, in_specs=in_specs, out_specs=out_specs, check_vma=False)
```

```python
import functools

import jax
import jax.numpy as jnp
from jax import lax
from jax.experimental import pallas as pl
from jax.experimental.pallas import tpu as pltpu
from jax.sharding import PartitionSpec as P

MESH = pl.DeviceIdType.MESH
F32 = jnp.float32
BF16 = jnp.bfloat16
CHUNKS = 4
GROUP = 2
UNROLL = 16
AHEAD = 1


def split(value):
    high = value.astype(BF16)
    low = (value - high.astype(F32)).astype(BF16)
    return high, low


def stack(value):
    high = value.astype(BF16).astype(F32)
    return jnp.concatenate([high, value - high], axis=0).astype(BF16)


def hit_matrix(labels, count, blocks):
    slots = labels.shape[1]
    slot = lax.broadcasted_iota(jnp.int32, (blocks, slots), 1)
    block = lax.broadcasted_iota(jnp.int32, (blocks, slots), 0)
    hits = jnp.where((slot < count) & (block == jnp.broadcast_to(labels, (blocks, slots))), 1.0, 0.0).astype(BF16)
    return jnp.concatenate([hits, hits], axis=1)


def kernel(
    rows_ref, cols_ref, count_ref, x_ref, tiles_ref, out_ref,
    rows_s, cols_s, count_s, rows_v, cols_v, raw, both, col_x, row_x, col_lhs, row_lhs, row_terms, col_terms, row_part, col_part, row_in, col_in,
    small_sem, tile_sem, colx_send, colx_recv, rowx_send, rowx_recv, rowp_send, rowp_recv, colp_send, colp_recv,
):
    row_devices = lax.axis_size("row")
    column_devices = lax.axis_size("col")
    r = lax.axis_index("row")
    c = lax.axis_index("col")
    vecs, width = x_ref.shape
    slots, side, _ = tiles_ref.shape
    local = width // side
    row_blocks = column_devices * local
    col_blocks = row_devices * local
    chunk = slots // CHUNKS
    stride = GROUP * UNROLL
    span = local * vecs
    most = (slots * (r + 1) + row_devices - 1) // row_devices
    steps = (most + stride - 1) // stride
    chunks = steps * (stride // chunk)

    row_peers = [(lax.rem(r + d, row_devices), c) for d in range(1, row_devices)]
    col_peers = [(r, lax.rem(c + d, column_devices)) for d in range(1, column_devices)]

    barrier = pltpu.get_barrier_semaphore()
    for peer in row_peers + col_peers:
        pl.semaphore_signal(barrier, inc=1, device_id=peer, device_id_type=MESH)

    def fetch(n):
        piece = pl.ds(n * chunk, chunk)
        return pltpu.make_async_copy(tiles_ref.at[piece], raw.at[piece], tile_sem.at[n])

    def begin(n, carry):
        fetch(n).start()
        return carry

    lax.fori_loop(0, chunks, begin, 0)
    pl.semaphore_wait(barrier, len(row_peers) + len(col_peers))

    colx, rowx, arrivals = [], [], []
    for n, peer in enumerate(row_peers):
        colx.append(pltpu.make_async_remote_copy(
            src_ref=x_ref, dst_ref=col_x.at[r], send_sem=colx_send.at[n], recv_sem=colx_recv.at[n],
            device_id=peer, device_id_type=MESH))
    for n in range(column_devices - 1):
        turn = 0 if n == 0 else lax.rem(c + column_devices - 2 + n, column_devices - 1) + 1
        other = jnp.where(c == 0, n + 1, turn)
        rowx.append(pltpu.make_async_remote_copy(
            src_ref=x_ref, dst_ref=row_x.at[c], send_sem=rowx_send.at[n], recv_sem=rowx_recv.at[c],
            device_id=(r, other), device_id_type=MESH))
        arrivals.append(pltpu.make_async_remote_copy(
            src_ref=x_ref, dst_ref=row_x.at[other], send_sem=rowx_send.at[n], recv_sem=rowx_recv.at[other],
            device_id=(r, other), device_id_type=MESH))
    for copy in rowx[:1] + colx + rowx[1:]:
        copy.start()

    smalls = [
        pltpu.make_async_copy(source, target, small_sem.at[n])
        for n, (source, target) in enumerate([
            (rows_ref, rows_v), (cols_ref, cols_v), (count_ref, count_s), (rows_ref, rows_s), (cols_ref, cols_s),
            (x_ref, col_x.at[r]), (x_ref, row_x.at[c]),
        ])
    ]
    for copy in smalls:
        copy.start()
    for copy in smalls:
        copy.wait()
    row_terms[...] = jnp.zeros_like(row_terms)
    col_terms[...] = jnp.zeros_like(col_terms)

    def halve(n, carry):
        fetch(n).wait()

        def one(i, carry):
            t = n * chunk + i
            high, low = split(raw[t])
            place = pl.ds(pl.multiple_of(t * side, side), side)
            both[place, 0:side] = high
            both[place, side:] = low
            return carry

        return lax.fori_loop(0, chunk, one, carry, unroll=8)

    lax.fori_loop(0, chunks, halve, 0)

    count = count_s[0, 0]
    row_hits = hit_matrix(rows_v[...], count, row_blocks)
    col_hits = hit_matrix(cols_v[...], count, col_blocks)

    for copy in colx:
        copy.wait()
    for i in range(row_devices):
        for j in range(local):
            n = i * local + j
            piece = stack(col_x[i, :, j * side:(j + 1) * side])
            col_lhs[n, :, 0:side] = piece
            col_lhs[n, :, side:] = piece

    def add_up(hits, terms, part):
        blocks = hits.shape[0]
        for k in range(0, vecs, 2):
            halves = [split(terms[pl.ds(k + m, slots, stride=vecs), :]) for m in range(2)]
            stacked = jnp.concatenate([jnp.concatenate(half, axis=0) for half in halves], axis=1)
            total = jnp.dot(hits, stacked, preferred_element_type=F32)
            for m in range(2):
                part[pl.ds(k + m, blocks, stride=vecs), :] = total[:, m * side:(m + 1) * side]

    def first(step, carry):
        for u in range(UNROLL):
            quad = step * UNROLL + u
            lhs = jnp.concatenate([col_lhs[cols_s[0, GROUP * quad + q]] for q in range(GROUP)], axis=0)
            rhs = both[pl.ds(pl.multiple_of(quad * GROUP * side, GROUP * side), GROUP * side), :]
            got = lax.dot_general(lhs, rhs, (((1,), (1,)), ((), ())), preferred_element_type=F32)
            place = pl.multiple_of(quad * GROUP * vecs, GROUP * vecs)
            for q in range(GROUP):
                own = got[2 * q * vecs:2 * (q + 1) * vecs, q * side:(q + 1) * side]
                row_terms[pl.ds(place + q * vecs, vecs), :] = own[0:vecs] + own[vecs:]
        return carry

    rowp = []
    for n, peer in enumerate(col_peers):
        rowp.append(pltpu.make_async_remote_copy(
            src_ref=row_part.at[pl.ds(pl.multiple_of(peer[1] * span, span), span)], dst_ref=row_in.at[n],
            send_sem=rowp_send.at[n], recv_sem=rowp_recv.at[n], device_id=peer, device_id_type=MESH))

    def finish_rows():
        add_up(row_hits, row_terms, row_part)
        for copy in rowp:
            copy.start()

    late = jnp.logical_and(2 * r >= row_devices, c == 0)
    ahead = jnp.where(late, jnp.minimum(steps, AHEAD), steps)
    lax.fori_loop(0, ahead, first, 0)
    pl.when(jnp.logical_not(late))(finish_rows)

    for sent, arrival in zip(rowx, arrivals):
        sent.wait_send()
        arrival.wait_recv()
    for i in range(column_devices):
        for j in range(local):
            row_lhs[i * local + j] = stack(row_x[i, :, j * side:(j + 1) * side])

    def second(step, carry):
        blank = jnp.zeros((2 * vecs, side), BF16)
        for u in range(UNROLL):
            quad = step * UNROLL + u
            parts = [row_lhs[rows_s[0, GROUP * quad + q]] for q in range(GROUP)]
            lhs = jnp.concatenate([
                jnp.concatenate([part, blank] if q % 2 == 0 else [blank, part], axis=1)
                for q, part in enumerate(parts)
            ], axis=0)
            start = pl.multiple_of(quad * GROUP * side, GROUP * side)
            rhs = jnp.concatenate([
                both[pl.ds(start + 2 * h * side, 2 * side), :] for h in range(GROUP // 2)
            ], axis=1)
            got = jnp.dot(lhs, rhs, preferred_element_type=F32)
            place = pl.multiple_of(quad * GROUP * vecs, GROUP * vecs)
            for q in range(GROUP):
                h = q // 2
                own = got[2 * q * vecs:2 * (q + 1) * vecs, 2 * h * side:2 * (h + 1) * side]
                own = own[0:vecs] + own[vecs:]
                col_terms[pl.ds(place + q * vecs, vecs), :] = own[:, 0:side] + own[:, side:]
        return carry

    lax.fori_loop(0, steps, second, 0)
    add_up(col_hits, col_terms, col_part)
    colp = []
    for n, peer in enumerate(row_peers):
        colp.append(pltpu.make_async_remote_copy(
            src_ref=col_part.at[pl.ds(pl.multiple_of(peer[0] * span, span), span)], dst_ref=col_in.at[n],
            send_sem=colp_send.at[n], recv_sem=colp_recv.at[n], device_id=peer, device_id_type=MESH))
        colp[-1].start()

    lax.fori_loop(ahead, steps, first, 0)
    pl.when(late)(finish_rows)

    total = row_part[pl.ds(pl.multiple_of(c * span, span), span)] + col_part[pl.ds(pl.multiple_of(r * span, span), span)]
    for n, copy in enumerate(rowp):
        copy.wait()
        total += row_in[n]
    for n, copy in enumerate(colp):
        copy.wait()
        total += col_in[n]
    for j in range(local):
        out_ref[:, j * side:(j + 1) * side] = total[j * vecs:(j + 1) * vecs]


def body(tiles, tile_rows, tile_cols, tile_counts, vectors):
    vecs, width = vectors.shape
    slots, side = tiles.shape[2:4]
    row_devices = lax.axis_size("row")
    column_devices = lax.axis_size("col")
    local = width // side
    row_blocks = column_devices * local
    col_blocks = row_devices * local
    rows = tile_rows.reshape(1, slots)
    cols = tile_cols.reshape(1, slots)
    vmem = pl.BlockSpec(memory_space=pltpu.VMEM)
    dma = pltpu.SemaphoreType.DMA
    return pl.pallas_call(
        kernel,
        out_shape=pltpu.VMEM((vecs, width), F32),
        in_specs=[pl.BlockSpec(memory_space=pltpu.HBM)] * 5,
        out_specs=vmem,
        scratch_shapes=[
            pltpu.SMEM((1, slots), jnp.int32),
            pltpu.SMEM((1, slots), jnp.int32),
            pltpu.SMEM((1, 1), jnp.int32),
            pltpu.VMEM((1, slots), jnp.int32),
            pltpu.VMEM((1, slots), jnp.int32),
            pltpu.VMEM((slots, side, side), F32),
            pltpu.VMEM((slots * side, 2 * side), BF16),
            pltpu.VMEM((row_devices, vecs, width), F32),
            pltpu.VMEM((column_devices, vecs, width), F32),
            pltpu.VMEM((col_blocks, 2 * vecs, 2 * side), BF16),
            pltpu.VMEM((row_blocks, 2 * vecs, side), BF16),
            pltpu.VMEM((slots * vecs, side), F32),
            pltpu.VMEM((slots * vecs, side), F32),
            pltpu.VMEM((row_blocks * vecs, side), F32),
            pltpu.VMEM((col_blocks * vecs, side), F32),
            pltpu.VMEM((column_devices - 1, local * vecs, side), F32),
            pltpu.VMEM((row_devices - 1, local * vecs, side), F32),
            dma((7,)),
            dma((CHUNKS,)),
            dma((row_devices - 1,)),
            dma((row_devices - 1,)),
            dma((column_devices - 1,)),
            dma((column_devices,)),
            dma((column_devices - 1,)),
            dma((column_devices - 1,)),
            dma((row_devices - 1,)),
            dma((row_devices - 1,)),
        ],
        compiler_params=pltpu.CompilerParams(
            collective_id=0, has_side_effects=True, vmem_limit_bytes=56 * 2**20
        ),
        cost_estimate=pl.CostEstimate(
            flops=12 * slots * side * side * vecs, bytes_accessed=4 * slots * side * side, transcendentals=0
        ),
        name="symmetric_product",
    )(rows, cols, tile_counts, vectors, tiles.reshape(slots, side, side))


def solution(mesh):
    in_specs = (
        P("row", "col", None, None, None),
        P("row", "col", None),
        P("row", "col", None),
        P("row", "col"),
        P(None, ("row", "col")),
    )
    out_specs = P(None, ("row", "col"))
    return jax.shard_map(body, mesh=mesh, in_specs=in_specs, out_specs=out_specs, check_vma=False)
```

```python
import functools

import jax
import jax.numpy as jnp
from jax import lax
from jax.experimental import pallas as pl
from jax.experimental.pallas import tpu as pltpu
from jax.sharding import PartitionSpec as P

MESH = pl.DeviceIdType.MESH
F32 = jnp.float32
BF16 = jnp.bfloat16
CHUNKS = 4
GROUP = 2
UNROLL = 16
AHEAD = 1


def split(value):
    high = value.astype(BF16)
    low = (value - high.astype(F32)).astype(BF16)
    return high, low


def stack(value):
    high = value.astype(BF16).astype(F32)
    return jnp.concatenate([high, value - high], axis=0).astype(BF16)


def hit_matrix(labels, count, blocks):
    slots = labels.shape[1]
    slot = lax.broadcasted_iota(jnp.int32, (blocks, slots), 1)
    block = lax.broadcasted_iota(jnp.int32, (blocks, slots), 0)
    hits = jnp.where((slot < count) & (block == jnp.broadcast_to(labels, (blocks, slots))), 1.0, 0.0).astype(BF16)
    return jnp.concatenate([hits, hits], axis=1)


def kernel(
    rows_ref, cols_ref, count_ref, x_ref, tiles_ref, out_ref,
    rows_s, cols_s, count_s, rows_v, cols_v, raw, both, col_x, row_x, col_lhs, row_lhs, row_terms, col_terms, row_part, col_part, row_in, col_in,
    small_sem, tile_sem, colx_send, colx_recv, rowx_send, rowx_recv, rowp_send, rowp_recv, colp_send, colp_recv,
):
    row_devices = lax.axis_size("row")
    column_devices = lax.axis_size("col")
    r = lax.axis_index("row")
    c = lax.axis_index("col")
    vecs, width = x_ref.shape
    slots, side, _ = tiles_ref.shape
    local = width // side
    row_blocks = column_devices * local
    col_blocks = row_devices * local
    chunk = slots // CHUNKS
    stride = GROUP * UNROLL
    span = local * vecs
    most = (slots * (r + 1) + row_devices - 1) // row_devices
    steps = (most + stride - 1) // stride
    chunks = steps * (stride // chunk)

    row_peers = [(lax.rem(r + d, row_devices), c) for d in range(1, row_devices)]
    col_peers = [(r, lax.rem(c + d, column_devices)) for d in range(1, column_devices)]

    barrier = pltpu.get_barrier_semaphore()
    for peer in row_peers + col_peers:
        pl.semaphore_signal(barrier, inc=1, device_id=peer, device_id_type=MESH)

    def fetch(n):
        piece = pl.ds(n * chunk, chunk)
        return pltpu.make_async_copy(tiles_ref.at[piece], raw.at[piece], tile_sem.at[n])

    def begin(n, carry):
        fetch(n).start()
        return carry

    lax.fori_loop(0, chunks, begin, 0)
    def halve(n, carry):
        fetch(n).wait()

        def one(i, carry):
            t = n * chunk + i
            high, low = split(raw[t])
            place = pl.ds(pl.multiple_of(t * side, side), side)
            both[place, 0:side] = high
            both[place, side:] = low
            return carry

        return lax.fori_loop(0, chunk, one, carry, unroll=8)

    early = jnp.where(c == 0, chunks, 0)
    lax.fori_loop(0, early, halve, 0)
    pl.semaphore_wait(barrier, len(row_peers) + len(col_peers))

    colx, rowx, arrivals = [], [], []
    for n, peer in enumerate(row_peers):
        colx.append(pltpu.make_async_remote_copy(
            src_ref=x_ref, dst_ref=col_x.at[r], send_sem=colx_send.at[n], recv_sem=colx_recv.at[n],
            device_id=peer, device_id_type=MESH))
    for n in range(column_devices - 1):
        turn = 0 if n == 0 else lax.rem(c + column_devices - 2 + n, column_devices - 1) + 1
        other = jnp.where(c == 0, n + 1, turn)
        rowx.append(pltpu.make_async_remote_copy(
            src_ref=x_ref, dst_ref=row_x.at[c], send_sem=rowx_send.at[n], recv_sem=rowx_recv.at[c],
            device_id=(r, other), device_id_type=MESH))
        arrivals.append(pltpu.make_async_remote_copy(
            src_ref=x_ref, dst_ref=row_x.at[other], send_sem=rowx_send.at[n], recv_sem=rowx_recv.at[other],
            device_id=(r, other), device_id_type=MESH))
    for copy in rowx[:1] + colx + rowx[1:]:
        copy.start()

    smalls = [
        pltpu.make_async_copy(source, target, small_sem.at[n])
        for n, (source, target) in enumerate([
            (rows_ref, rows_v), (cols_ref, cols_v), (count_ref, count_s), (rows_ref, rows_s), (cols_ref, cols_s),
            (x_ref, col_x.at[r]), (x_ref, row_x.at[c]),
        ])
    ]
    for copy in smalls:
        copy.start()
    row_terms[...] = jnp.zeros_like(row_terms)
    col_terms[...] = jnp.zeros_like(col_terms)

    lax.fori_loop(early, chunks, halve, 0)

    for copy in smalls:
        copy.wait()
    count = count_s[0, 0]
    row_hits = hit_matrix(rows_v[...], count, row_blocks)
    col_hits = hit_matrix(cols_v[...], count, col_blocks)

    for copy in colx:
        copy.wait()
    for i in range(row_devices):
        for j in range(local):
            n = i * local + j
            piece = stack(col_x[i, :, j * side:(j + 1) * side])
            col_lhs[n, :, 0:side] = piece
            col_lhs[n, :, side:] = piece

    def add_up(hits, terms, part):
        blocks = hits.shape[0]
        for k in range(0, vecs, 2):
            halves = [split(terms[pl.ds(k + m, slots, stride=vecs), :]) for m in range(2)]
            stacked = jnp.concatenate([jnp.concatenate(half, axis=0) for half in halves], axis=1)
            total = jnp.dot(hits, stacked, preferred_element_type=F32)
            for m in range(2):
                part[pl.ds(k + m, blocks, stride=vecs), :] = total[:, m * side:(m + 1) * side]

    def first(step, carry):
        for u in range(UNROLL):
            quad = step * UNROLL + u
            lhs = jnp.concatenate([col_lhs[cols_s[0, GROUP * quad + q]] for q in range(GROUP)], axis=0)
            rhs = both[pl.ds(pl.multiple_of(quad * GROUP * side, GROUP * side), GROUP * side), :]
            got = lax.dot_general(lhs, rhs, (((1,), (1,)), ((), ())), preferred_element_type=F32)
            place = pl.multiple_of(quad * GROUP * vecs, GROUP * vecs)
            for q in range(GROUP):
                own = got[2 * q * vecs:2 * (q + 1) * vecs, q * side:(q + 1) * side]
                row_terms[pl.ds(place + q * vecs, vecs), :] = own[0:vecs] + own[vecs:]
        return carry

    rowp = []
    for n, peer in enumerate(col_peers):
        rowp.append(pltpu.make_async_remote_copy(
            src_ref=row_part.at[pl.ds(pl.multiple_of(peer[1] * span, span), span)], dst_ref=row_in.at[n],
            send_sem=rowp_send.at[n], recv_sem=rowp_recv.at[n], device_id=peer, device_id_type=MESH))

    def finish_rows():
        add_up(row_hits, row_terms, row_part)
        for copy in rowp:
            copy.start()

    late = jnp.logical_and(2 * r >= row_devices, c == 0)
    ahead = jnp.where(late, jnp.minimum(steps, AHEAD), steps)
    lax.fori_loop(0, ahead, first, 0)
    pl.when(jnp.logical_not(late))(finish_rows)

    for sent, arrival in zip(rowx, arrivals):
        sent.wait_send()
        arrival.wait_recv()
    for i in range(column_devices):
        for j in range(local):
            row_lhs[i * local + j] = stack(row_x[i, :, j * side:(j + 1) * side])

    def second(step, carry):
        blank = jnp.zeros((2 * vecs, side), BF16)
        for u in range(UNROLL):
            quad = step * UNROLL + u
            parts = [row_lhs[rows_s[0, GROUP * quad + q]] for q in range(GROUP)]
            lhs = jnp.concatenate([
                jnp.concatenate([part, blank] if q % 2 == 0 else [blank, part], axis=1)
                for q, part in enumerate(parts)
            ], axis=0)
            start = pl.multiple_of(quad * GROUP * side, GROUP * side)
            rhs = jnp.concatenate([
                both[pl.ds(start + 2 * h * side, 2 * side), :] for h in range(GROUP // 2)
            ], axis=1)
            got = jnp.dot(lhs, rhs, preferred_element_type=F32)
            place = pl.multiple_of(quad * GROUP * vecs, GROUP * vecs)
            for q in range(GROUP):
                h = q // 2
                own = got[2 * q * vecs:2 * (q + 1) * vecs, 2 * h * side:2 * (h + 1) * side]
                own = own[0:vecs] + own[vecs:]
                col_terms[pl.ds(place + q * vecs, vecs), :] = own[:, 0:side] + own[:, side:]
        return carry

    lax.fori_loop(0, steps, second, 0)
    add_up(col_hits, col_terms, col_part)
    colp = []
    for n, peer in enumerate(row_peers):
        colp.append(pltpu.make_async_remote_copy(
            src_ref=col_part.at[pl.ds(pl.multiple_of(peer[0] * span, span), span)], dst_ref=col_in.at[n],
            send_sem=colp_send.at[n], recv_sem=colp_recv.at[n], device_id=peer, device_id_type=MESH))
        colp[-1].start()

    lax.fori_loop(ahead, steps, first, 0)
    pl.when(late)(finish_rows)

    total = row_part[pl.ds(pl.multiple_of(c * span, span), span)] + col_part[pl.ds(pl.multiple_of(r * span, span), span)]
    for n, copy in enumerate(rowp):
        copy.wait()
        total += row_in[n]
    for n, copy in enumerate(colp):
        copy.wait()
        total += col_in[n]
    for j in range(local):
        out_ref[:, j * side:(j + 1) * side] = total[j * vecs:(j + 1) * vecs]


def body(tiles, tile_rows, tile_cols, tile_counts, vectors):
    vecs, width = vectors.shape
    slots, side = tiles.shape[2:4]
    row_devices = lax.axis_size("row")
    column_devices = lax.axis_size("col")
    local = width // side
    row_blocks = column_devices * local
    col_blocks = row_devices * local
    rows = tile_rows.reshape(1, slots)
    cols = tile_cols.reshape(1, slots)
    vmem = pl.BlockSpec(memory_space=pltpu.VMEM)
    dma = pltpu.SemaphoreType.DMA
    return pl.pallas_call(
        kernel,
        out_shape=pltpu.VMEM((vecs, width), F32),
        in_specs=[pl.BlockSpec(memory_space=pltpu.HBM)] * 5,
        out_specs=vmem,
        scratch_shapes=[
            pltpu.SMEM((1, slots), jnp.int32),
            pltpu.SMEM((1, slots), jnp.int32),
            pltpu.SMEM((1, 1), jnp.int32),
            pltpu.VMEM((1, slots), jnp.int32),
            pltpu.VMEM((1, slots), jnp.int32),
            pltpu.VMEM((slots, side, side), F32),
            pltpu.VMEM((slots * side, 2 * side), BF16),
            pltpu.VMEM((row_devices, vecs, width), F32),
            pltpu.VMEM((column_devices, vecs, width), F32),
            pltpu.VMEM((col_blocks, 2 * vecs, 2 * side), BF16),
            pltpu.VMEM((row_blocks, 2 * vecs, side), BF16),
            pltpu.VMEM((slots * vecs, side), F32),
            pltpu.VMEM((slots * vecs, side), F32),
            pltpu.VMEM((row_blocks * vecs, side), F32),
            pltpu.VMEM((col_blocks * vecs, side), F32),
            pltpu.VMEM((column_devices - 1, local * vecs, side), F32),
            pltpu.VMEM((row_devices - 1, local * vecs, side), F32),
            dma((7,)),
            dma((CHUNKS,)),
            dma((row_devices - 1,)),
            dma((row_devices - 1,)),
            dma((column_devices - 1,)),
            dma((column_devices,)),
            dma((column_devices - 1,)),
            dma((column_devices - 1,)),
            dma((row_devices - 1,)),
            dma((row_devices - 1,)),
        ],
        compiler_params=pltpu.CompilerParams(
            collective_id=0, has_side_effects=True, vmem_limit_bytes=56 * 2**20
        ),
        cost_estimate=pl.CostEstimate(
            flops=12 * slots * side * side * vecs, bytes_accessed=4 * slots * side * side, transcendentals=0
        ),
        name="symmetric_product",
    )(rows, cols, tile_counts, vectors, tiles.reshape(slots, side, side))


def solution(mesh):
    in_specs = (
        P("row", "col", None, None, None),
        P("row", "col", None),
        P("row", "col", None),
        P("row", "col"),
        P(None, ("row", "col")),
    )
    out_specs = P(None, ("row", "col"))
    return jax.shard_map(body, mesh=mesh, in_specs=in_specs, out_specs=out_specs, check_vma=False)
```

```python
import functools

import jax
import jax.numpy as jnp
from jax import lax
from jax.experimental import pallas as pl
from jax.experimental.pallas import tpu as pltpu
from jax.sharding import PartitionSpec as P

MESH = pl.DeviceIdType.MESH
F32 = jnp.float32
BF16 = jnp.bfloat16
CHUNKS = 4
GROUP = 2
UNROLL = 16
AHEAD = 3


def split(value):
    high = value.astype(BF16)
    low = (value - high.astype(F32)).astype(BF16)
    return high, low


def stack(value):
    high = value.astype(BF16).astype(F32)
    return jnp.concatenate([high, value - high], axis=0).astype(BF16)


def hit_matrix(labels, count, blocks):
    slots = labels.shape[1]
    slot = lax.broadcasted_iota(jnp.int32, (blocks, slots), 1)
    block = lax.broadcasted_iota(jnp.int32, (blocks, slots), 0)
    hits = jnp.where((slot < count) & (block == jnp.broadcast_to(labels, (blocks, slots))), 1.0, 0.0).astype(BF16)
    return jnp.concatenate([hits, hits], axis=1)


def kernel(
    rows_ref, cols_ref, count_ref, x_ref, tiles_ref, out_ref,
    rows_s, cols_s, count_s, rows_v, cols_v, raw, both, col_x, row_x, col_lhs, row_lhs, row_terms, col_terms, row_part, col_part, row_in, col_in,
    small_sem, tile_sem, colx_send, colx_recv, rowx_send, rowx_recv, rowp_send, rowp_recv, colp_send, colp_recv,
):
    row_devices = lax.axis_size("row")
    column_devices = lax.axis_size("col")
    r = lax.axis_index("row")
    c = lax.axis_index("col")
    vecs, width = x_ref.shape
    slots, side, _ = tiles_ref.shape
    local = width // side
    row_blocks = column_devices * local
    col_blocks = row_devices * local
    chunk = slots // CHUNKS
    stride = GROUP * UNROLL
    span = local * vecs
    most = (slots * (r + 1) + row_devices - 1) // row_devices
    steps = (most + stride - 1) // stride
    chunks = steps * (stride // chunk)

    row_peers = [(lax.rem(r + d, row_devices), c) for d in range(1, row_devices)]
    col_peers = [(r, lax.rem(c + d, column_devices)) for d in range(1, column_devices)]

    barrier = pltpu.get_barrier_semaphore()
    for peer in row_peers + col_peers:
        pl.semaphore_signal(barrier, inc=1, device_id=peer, device_id_type=MESH)

    def fetch(n):
        piece = pl.ds(n * chunk, chunk)
        return pltpu.make_async_copy(tiles_ref.at[piece], raw.at[piece], tile_sem.at[n])

    def begin(n, carry):
        fetch(n).start()
        return carry

    lax.fori_loop(0, chunks, begin, 0)

    def halve(n, carry):
        fetch(n).wait()

        def one(i, carry):
            t = n * chunk + i
            high, low = split(raw[t])
            place = pl.ds(pl.multiple_of(t * side, side), side)
            both[place, 0:side] = high
            both[place, side:] = low
            return carry

        return lax.fori_loop(0, chunk, one, carry, unroll=8)

    early = jnp.where(c == 0, chunks, 0)
    lax.fori_loop(0, early, halve, 0)
    pl.semaphore_wait(barrier, len(row_peers) + len(col_peers))

    colx, rowx, arrivals = [], [], []
    for n, peer in enumerate(row_peers):
        colx.append(pltpu.make_async_remote_copy(
            src_ref=x_ref, dst_ref=col_x.at[r], send_sem=colx_send.at[n], recv_sem=colx_recv.at[n],
            device_id=peer, device_id_type=MESH))
    for n in range(column_devices - 1):
        turn = 0 if n == 0 else lax.rem(c + column_devices - 2 + n, column_devices - 1) + 1
        other = jnp.where(c == 0, n + 1, turn)
        rowx.append(pltpu.make_async_remote_copy(
            src_ref=x_ref, dst_ref=row_x.at[c], send_sem=rowx_send.at[n], recv_sem=rowx_recv.at[c],
            device_id=(r, other), device_id_type=MESH))
        arrivals.append(pltpu.make_async_remote_copy(
            src_ref=x_ref, dst_ref=row_x.at[other], send_sem=rowx_send.at[n], recv_sem=rowx_recv.at[other],
            device_id=(r, other), device_id_type=MESH))
    for copy in rowx[:1] + colx + rowx[1:]:
        copy.start()

    smalls = [
        pltpu.make_async_copy(source, target, small_sem.at[n])
        for n, (source, target) in enumerate([
            (rows_ref, rows_v), (cols_ref, cols_v), (count_ref, count_s), (rows_ref, rows_s), (cols_ref, cols_s),
            (x_ref, col_x.at[r]), (x_ref, row_x.at[c]),
        ])
    ]
    for copy in smalls:
        copy.start()
    row_terms[...] = jnp.zeros_like(row_terms)
    col_terms[...] = jnp.zeros_like(col_terms)

    lax.fori_loop(early, chunks, halve, 0)

    for copy in smalls:
        copy.wait()
    count = count_s[0, 0]
    row_hits = hit_matrix(rows_v[...], count, row_blocks)
    col_hits = hit_matrix(cols_v[...], count, col_blocks)

    for copy in colx:
        copy.wait()
    for i in range(row_devices):
        for j in range(local):
            n = i * local + j
            piece = stack(col_x[i, :, j * side:(j + 1) * side])
            col_lhs[n, :, 0:side] = piece
            col_lhs[n, :, side:] = piece

    def add_up(hits, terms, part):
        blocks = hits.shape[0]
        for k in range(0, vecs, 2):
            halves = [split(terms[pl.ds(k + m, slots, stride=vecs), :]) for m in range(2)]
            stacked = jnp.concatenate([jnp.concatenate(half, axis=0) for half in halves], axis=1)
            total = jnp.dot(hits, stacked, preferred_element_type=F32)
            for m in range(2):
                part[pl.ds(k + m, blocks, stride=vecs), :] = total[:, m * side:(m + 1) * side]

    def first(step, carry):
        for u in range(UNROLL):
            quad = step * UNROLL + u
            lhs = jnp.concatenate([col_lhs[cols_s[0, GROUP * quad + q]] for q in range(GROUP)], axis=0)
            rhs = both[pl.ds(pl.multiple_of(quad * GROUP * side, GROUP * side), GROUP * side), :]
            got = lax.dot_general(lhs, rhs, (((1,), (1,)), ((), ())), preferred_element_type=F32)
            place = pl.multiple_of(quad * GROUP * vecs, GROUP * vecs)
            for q in range(GROUP):
                own = got[2 * q * vecs:2 * (q + 1) * vecs, q * side:(q + 1) * side]
                row_terms[pl.ds(place + q * vecs, vecs), :] = own[0:vecs] + own[vecs:]
        return carry

    rowp = []
    for n, peer in enumerate(col_peers):
        rowp.append(pltpu.make_async_remote_copy(
            src_ref=row_part.at[pl.ds(pl.multiple_of(peer[1] * span, span), span)], dst_ref=row_in.at[n],
            send_sem=rowp_send.at[n], recv_sem=rowp_recv.at[n], device_id=peer, device_id_type=MESH))

    def finish_rows():
        add_up(row_hits, row_terms, row_part)
        for copy in rowp:
            copy.start()

    late = jnp.logical_and(2 * r >= row_devices, c == 0)
    ahead = jnp.where(late, jnp.minimum(steps, AHEAD), steps)
    lax.fori_loop(0, ahead, first, 0)
    pl.when(jnp.logical_not(late))(finish_rows)

    for sent, arrival in zip(rowx, arrivals):
        sent.wait_send()
        arrival.wait_recv()
    for i in range(column_devices):
        for j in range(local):
            row_lhs[i * local + j] = stack(row_x[i, :, j * side:(j + 1) * side])

    def second(step, carry):
        blank = jnp.zeros((2 * vecs, side), BF16)
        for u in range(UNROLL):
            quad = step * UNROLL + u
            parts = [row_lhs[rows_s[0, GROUP * quad + q]] for q in range(GROUP)]
            lhs = jnp.concatenate([
                jnp.concatenate([part, blank] if q % 2 == 0 else [blank, part], axis=1)
                for q, part in enumerate(parts)
            ], axis=0)
            start = pl.multiple_of(quad * GROUP * side, GROUP * side)
            rhs = jnp.concatenate([
                both[pl.ds(start + 2 * h * side, 2 * side), :] for h in range(GROUP // 2)
            ], axis=1)
            got = jnp.dot(lhs, rhs, preferred_element_type=F32)
            place = pl.multiple_of(quad * GROUP * vecs, GROUP * vecs)
            for q in range(GROUP):
                h = q // 2
                own = got[2 * q * vecs:2 * (q + 1) * vecs, 2 * h * side:2 * (h + 1) * side]
                own = own[0:vecs] + own[vecs:]
                col_terms[pl.ds(place + q * vecs, vecs), :] = own[:, 0:side] + own[:, side:]
        return carry

    lax.fori_loop(0, steps, second, 0)
    add_up(col_hits, col_terms, col_part)
    colp = []
    for n, peer in enumerate(row_peers):
        colp.append(pltpu.make_async_remote_copy(
            src_ref=col_part.at[pl.ds(pl.multiple_of(peer[0] * span, span), span)], dst_ref=col_in.at[n],
            send_sem=colp_send.at[n], recv_sem=colp_recv.at[n], device_id=peer, device_id_type=MESH))
        colp[-1].start()

    lax.fori_loop(ahead, steps, first, 0)
    pl.when(late)(finish_rows)

    total = row_part[pl.ds(pl.multiple_of(c * span, span), span)] + col_part[pl.ds(pl.multiple_of(r * span, span), span)]
    for n, copy in enumerate(rowp):
        copy.wait()
        total += row_in[n]
    for n, copy in enumerate(colp):
        copy.wait()
        total += col_in[n]
    for j in range(local):
        out_ref[:, j * side:(j + 1) * side] = total[j * vecs:(j + 1) * vecs]


def body(tiles, tile_rows, tile_cols, tile_counts, vectors):
    vecs, width = vectors.shape
    slots, side = tiles.shape[2:4]
    row_devices = lax.axis_size("row")
    column_devices = lax.axis_size("col")
    local = width // side
    row_blocks = column_devices * local
    col_blocks = row_devices * local
    rows = tile_rows.reshape(1, slots)
    cols = tile_cols.reshape(1, slots)
    vmem = pl.BlockSpec(memory_space=pltpu.VMEM)
    dma = pltpu.SemaphoreType.DMA
    return pl.pallas_call(
        kernel,
        out_shape=pltpu.VMEM((vecs, width), F32),
        in_specs=[pl.BlockSpec(memory_space=pltpu.HBM)] * 5,
        out_specs=vmem,
        scratch_shapes=[
            pltpu.SMEM((1, slots), jnp.int32),
            pltpu.SMEM((1, slots), jnp.int32),
            pltpu.SMEM((1, 1), jnp.int32),
            pltpu.VMEM((1, slots), jnp.int32),
            pltpu.VMEM((1, slots), jnp.int32),
            pltpu.VMEM((slots, side, side), F32),
            pltpu.VMEM((slots * side, 2 * side), BF16),
            pltpu.VMEM((row_devices, vecs, width), F32),
            pltpu.VMEM((column_devices, vecs, width), F32),
            pltpu.VMEM((col_blocks, 2 * vecs, 2 * side), BF16),
            pltpu.VMEM((row_blocks, 2 * vecs, side), BF16),
            pltpu.VMEM((slots * vecs, side), F32),
            pltpu.VMEM((slots * vecs, side), F32),
            pltpu.VMEM((row_blocks * vecs, side), F32),
            pltpu.VMEM((col_blocks * vecs, side), F32),
            pltpu.VMEM((column_devices - 1, local * vecs, side), F32),
            pltpu.VMEM((row_devices - 1, local * vecs, side), F32),
            dma((7,)),
            dma((CHUNKS,)),
            dma((row_devices - 1,)),
            dma((row_devices - 1,)),
            dma((column_devices - 1,)),
            dma((column_devices,)),
            dma((column_devices - 1,)),
            dma((column_devices - 1,)),
            dma((row_devices - 1,)),
            dma((row_devices - 1,)),
        ],
        compiler_params=pltpu.CompilerParams(
            collective_id=0, has_side_effects=True, vmem_limit_bytes=56 * 2**20
        ),
        cost_estimate=pl.CostEstimate(
            flops=12 * slots * side * side * vecs, bytes_accessed=4 * slots * side * side, transcendentals=0
        ),
        name="symmetric_product",
    )(rows, cols, tile_counts, vectors, tiles.reshape(slots, side, side))


def solution(mesh):
    in_specs = (
        P("row", "col", None, None, None),
        P("row", "col", None),
        P("row", "col", None),
        P("row", "col"),
        P(None, ("row", "col")),
    )
    out_specs = P(None, ("row", "col"))
    return jax.shard_map(body, mesh=mesh, in_specs=in_specs, out_specs=out_specs, check_vma=False)
```
